32 devices in a mesh: elem: 8 (over z, x), band: 4 (over y, core).
Axes of the slice: x: 2, y: 2, z: 4, core: 2. Of those that a mesh axis runs over, the one named last changes fastest.
Arguments:
- basis_counts: int32 [64, 16], P('elem', 'band'), may hold values from 1 to 128, as said below
- neighbour_codes: int32 [64, 16, 6], P('elem', 'band'), may hold values from 0 to 8, as said below
- x_block: bfloat16 [64, 16, 160, 128], P('elem', 'band'), may hold values from -6 to 6
- h_self: bfloat16 [64, 16, 128, 128], P('elem', 'band'), may hold values from -0.375 to 0.375
- h_near: bfloat16 [64, 16, 6, 128, 128], P('elem', 'band'), may hold values from -0.375 to 0.375
Outputs:
- filtered: bfloat16 [64, 16, 160, 128], P('elem', 'band')
- gram: float32 [160, 160], P('band')
- ritz: float32 [160, 160], P('band')
The draws below stay inside these ranges and needn't reach their ends.
Inputs may be any that keep to these rules, and one draw needn't show every extreme that they name: `basis_counts`: at least one element holds exactly 128 basis functions. `neighbour_codes`: an element's 6 codes are distinct and never 4; code q names the element offset by q // 3 - 1 along the first dimension and q % 3 - 1 along the second, periodically.
All inputs are finite; a program needn't handle non-finite values.
Results may differ from the reference program's by a relative error of at most 0.007.
Values may be sent and summed in bfloat16 or wider, within the bound.
A program may use at most 128 MiB of HBM per device.

```python
import jax
import jax.numpy as jnp
from jax import lax

NB_MAX = 128
COLS = 160
K = 6
EX = 64
EY = 16
ELEMS = 1024


def draw_basis_counts(key, part):
    key_base, key_factor, key_pick = jax.random.split(key, 3)
    base = jax.random.randint(key_base, (EX, EY), 1, NB_MAX // 2 + 1)
    factor = jax.random.randint(key_factor, (EX, 1), 1, 4)
    counts = jnp.minimum(base * factor, NB_MAX).reshape(-1)
    pick = jax.random.randint(key_pick, (), 0, EX * EY)
    counts = counts.at[pick].set(NB_MAX)
    return counts.reshape(EX, EY).astype(jnp.int32)


def draw_neighbour_codes(key, part):
    scores = jax.random.randint(key, (EX, EY, 8), 0, 1 << 20) * 8 + jnp.arange(8, dtype=jnp.int32)
    order = jnp.argsort(scores, axis=-1)[:, :, :K]
    codes = order + (order >= 4).astype(jnp.int32)
    return codes.astype(jnp.int32)


def strengthened(array, own_key, source, target, parts, factor):
    owner, partner = [(jnp.arange(array.shape[position]) // (array.shape[position] // parts)).reshape([-1 if axis == position else 1 for axis in range(array.ndim)]) for position in (source, target)]
    chosen = jax.random.permutation(own_key, parts)[partner]
    strong = (owner == chosen) | (owner == (partner + parts // 2) % parts)
    return jnp.where(strong, factor * array, array)


def shard_levels(key, dims, shards, low, top_value):
    def one(axis_at, shards_of):
        steps = jax.random.uniform(jax.random.fold_in(jax.random.fold_in(key, 6), axis_at), (shards_of,), jnp.float32, low / len(shards), top_value / len(shards))
        return jnp.repeat(jnp.exp(steps), dims[axis_at] // shards_of).reshape((-1,) + (1,) * (len(dims) - axis_at - 1))

    level = one(*shards[0])
    for cut in shards[1:]:
        level = level * one(*cut)
    return level


def centred(own_key, dims, width, limit, pieces=(), kind=jnp.bfloat16):
    factor_of = shard_levels(own_key, dims, pieces, -0.22, 0.18) if pieces else 1.0
    array = jax.random.normal(own_key, dims, jnp.float32) * width * factor_of
    return jnp.minimum(jnp.maximum(array, -limit), limit).astype(kind)


def bell_draw_with(key, shape, scale, limit, shards, heavy, kind=jnp.bfloat16):
    drawn = scale * jax.random.normal(key, shape, jnp.float32)
    if shards:
        drawn = drawn * shard_levels(key, shape, shards, -0.22, 0.18)
    return jnp.clip(strengthened(drawn, jax.random.fold_in(key, 3), *heavy), -limit, limit).astype(kind)


def setup_inputs(seed: int = 0) -> dict:
    arg_keys = jax.random.split(jax.random.key(seed), 6)
    return {
        "basis_counts": draw_basis_counts(jax.random.fold_in(arg_keys[5], 71), 0),
        "neighbour_codes": draw_neighbour_codes(jax.random.fold_in(arg_keys[5], 71), 0),
        "x_block": bell_draw_with(arg_keys[2], (EX, EY, COLS, NB_MAX), 1.0, 6.0, ((0, 8), (1, 4)), (0, 2, 8, 2.0)),
        "h_self": centred(arg_keys[3], (EX, EY, NB_MAX, NB_MAX), ((K + 1) * NB_MAX // 3) ** -0.5, 0.375, ((0, 8), (1, 4))),
        "h_near": centred(arg_keys[4], (EX, EY, K, NB_MAX, NB_MAX), ((K + 1) * NB_MAX // 3) ** -0.5, 0.375, ((0, 8), (1, 4))),
    }


cheb_center = 0.25
cheb_half = 1.5


def operate(vector_block, h_self, h_near, neighbour_codes, live_mask):
    extended = jnp.pad(vector_block, ((1, 1), (1, 1), (0, 0), (0, 0)), mode="wrap")
    width_ext = EY + 2

    def one_row(packed):
        row_index, own_row, self_row, near_row, code_row, mask_row = packed
        window = lax.dynamic_slice_in_dim(extended, row_index, 3, 0).reshape(3 * width_ext, COLS, NB_MAX)
        gather_index = (code_row // 3) * width_ext + jnp.arange(EY, dtype=jnp.int32)[:, None] + code_row % 3
        nearby = jnp.take(window, gather_index.astype(jnp.int32), axis=0)
        summed = jnp.einsum("ecs,esr->ecr", own_row.astype(jnp.float32), self_row.astype(jnp.float32))
        summed = summed + jnp.einsum("ekcs,eksr->ecr", nearby.astype(jnp.float32), near_row.astype(jnp.float32))
        return jnp.where(mask_row, summed, jnp.float32(0.0))

    row_ids = jnp.arange(EX, dtype=jnp.int32)
    return lax.map(one_row, (row_ids, vector_block, h_self, h_near, neighbour_codes, live_mask))


def reference(basis_counts, neighbour_codes, x_block, h_self, h_near):
    live_mask = jnp.arange(NB_MAX, dtype=jnp.int32)[None, None, None, :] < basis_counts[:, :, None, None]
    start = jnp.where(live_mask, x_block, jnp.zeros_like(x_block))

    def apply_op(vector_block):
        return operate(vector_block, h_self, h_near, neighbour_codes, live_mask)

    first = ((apply_op(start) - cheb_center * start.astype(jnp.float32)) / cheb_half).astype(jnp.bfloat16)
    second = (2.0 * (apply_op(first) - cheb_center * first.astype(jnp.float32)) / cheb_half - start.astype(jnp.float32)).astype(jnp.bfloat16)
    filtered = (2.0 * (apply_op(second) - cheb_center * second.astype(jnp.float32)) / cheb_half - first.astype(jnp.float32)).astype(jnp.bfloat16)
    image = apply_op(filtered).astype(jnp.bfloat16)

    def accumulate(carry, packed):
        filt_row, image_row = packed
        left = filt_row.astype(jnp.float32)
        gram_part = jnp.einsum("ecr,edr->cd", left, left)
        ritz_part = jnp.einsum("ecr,edr->cd", left, image_row.astype(jnp.float32))
        return (carry[0] + gram_part, carry[1] + ritz_part), None

    zeros = jnp.zeros((COLS, COLS), jnp.float32)
    (gram_sum, ritz_sum), unused = lax.scan(accumulate, (zeros, zeros), (filtered, image))
    normalizer = jnp.float32(ELEMS * NB_MAX / 3.0)
    return filtered, gram_sum / normalizer, ritz_sum / normalizer
```

```python
import functools

import jax
import jax.numpy as jnp
from jax import lax
from jax.experimental import pallas as pl
from jax.experimental.pallas import tpu as pltpu
from jax.sharding import PartitionSpec as P

MESH = pl.DeviceIdType.MESH
cheb_center = 0.25
cheb_half = 1.5
steps = 4
halves = 2
directions = [(a, b) for a in (-1, 0, 1) for b in (-1, 0, 1) if (a, b) != (0, 0)]


def edge(shift, count):
    if shift == 0:
        return 1, 1, count
    return (count, 0, 1) if shift > 0 else (1, count + 1, 1)


def kernel(elem_count, band_count, counts, codes, x_ref, self_ref, near_ref, out_ref, gram_ref, ritz_ref, *scratch):
    exts = [scratch[step * halves : (step + 1) * halves] for step in range(steps)]
    blocks, images, send_sem, recv_sem, load_sem, out_sem = scratch[steps * halves :]
    rows, cols, neighbours = codes.shape
    columns, basis = x_ref.shape[2:]
    part = columns // halves
    depth = near_ref.shape[2]

    my_elem, my_band = lax.axis_index("elem"), lax.axis_index("band")
    partners = [
        (lax.rem(my_elem + a + elem_count, elem_count), lax.rem(my_band + b + band_count, band_count))
        for a, b in directions
    ]

    x_loads = [
        pltpu.make_async_copy(
            x_ref.at[:, :, pl.ds(half * part, part)],
            exts[0][half].at[pl.ds(1, rows), pl.ds(1, cols)],
            load_sem.at[half],
        )
        for half in range(halves)
    ]
    h_loads = [
        pltpu.make_async_copy(near_ref, blocks.at[:, :, pl.ds(0, depth)], load_sem.at[halves]),
        pltpu.make_async_copy(self_ref, blocks.at[:, :, pl.ds(depth, basis)], load_sem.at[halves + 1]),
    ]
    for copy in x_loads + h_loads:
        copy.start()

    barrier = pltpu.get_barrier_semaphore()
    for partner in partners:
        pl.semaphore_signal(barrier, inc=1, device_id=partner, device_id_type=MESH)
    pl.semaphore_wait(barrier, len(partners))

    lanes = lax.broadcasted_iota(jnp.int32, (part, basis), 1)

    def halo(step, half, which):
        a, b = directions[which]
        row_from, row_to, row_len = edge(a, rows)
        col_from, col_to, col_len = edge(b, cols)
        ext = exts[step][half]
        return pltpu.make_async_remote_copy(
            src_ref=ext.at[pl.ds(row_from, row_len), pl.ds(col_from, col_len)],
            dst_ref=ext.at[pl.ds(row_to, row_len), pl.ds(col_to, col_len)],
            send_sem=send_sem.at[step, half, which],
            recv_sem=recv_sem.at[step, half, which],
            device_id=partners[which],
            device_id_type=MESH,
        )

    vertical = [d for d, (a, b) in enumerate(directions) if a != 0]
    sideways = [d for d, (a, b) in enumerate(directions) if a == 0]

    for half in range(halves):
        x_loads[half].wait()
        ext = exts[0][half]

        def clear(row, carry, ext=ext):
            for col in range(cols):
                held = ext[row + 1, col + 1]
                ext[row + 1, col + 1] = jnp.where(
                    lanes < counts[row, col], held.astype(jnp.float32), 0.0
                ).astype(held.dtype)
            return carry

        lax.fori_loop(0, rows, clear, 0)
        for which in sideways + vertical:
            halo(0, half, which).start()

    def one_row(step, half, row):
        ext = exts[step][half]
        for col in range(cols):
            pieces = []
            for k in range(neighbours):
                code = codes[row, col, k]
                a = (code * 11) >> 5
                pieces.append(ext[row + a, col + code - 3 * a])
            own = ext[row + 1, col + 1]
            pieces.append(own)
            summed = jnp.dot(
                jnp.concatenate(pieces, axis=1), blocks[row, col], preferred_element_type=jnp.float32
            )
            if step < steps - 1:
                value = (summed - cheb_center * own.astype(jnp.float32)) * (
                    (1.0 if step == 0 else 2.0) / cheb_half
                )
                if step > 0:
                    value = value - exts[step - 1][half][row + 1, col + 1].astype(jnp.float32)
                value = jnp.where(lanes < counts[row, col], value, 0.0)
                exts[step + 1][half][row + 1, col + 1] = value.astype(own.dtype)
            else:
                value = jnp.where(lanes < counts[row, col], summed, 0.0)
                images[row, col, pl.ds(half * part, part)] = value.astype(own.dtype)

    def row_loop(first, count, stride, step, half):
        def body(i, carry):
            one_row(step, half, first + i * stride)
            return carry

        lax.fori_loop(0, count, body, 0)

    def wide(row):
        return jnp.concatenate(
            [
                jnp.concatenate([exts[steps - 1][half][row + 1, col + 1] for half in range(halves)], axis=0)
                for col in range(cols)
            ],
            axis=1,
        )

    contract = (((1,), (1,)), ((), ()))
    out_copies = []
    for step in range(steps):
        for half in range(halves):
            for which in range(len(directions)):
                halo(step, half, which).wait()
            if step == 0 and half == 0:
                for copy in h_loads:
                    copy.wait()
            row_loop(0, 2, rows - 1, step, half)
            if step < steps - 1:
                for which in vertical:
                    halo(step + 1, half, which).start()
            row_loop(1, rows - 2, 1, step, half)
            if step < steps - 1:
                for which in sideways:
                    halo(step + 1, half, which).start()
            if step == steps - 2:
                out_copies.append(
                    pltpu.make_async_copy(
                        exts[steps - 1][half].at[pl.ds(1, rows), pl.ds(1, cols)],
                        out_ref.at[:, :, pl.ds(half * part, part)],
                        out_sem.at[half],
                    )
                )
                out_copies[-1].start()
        if step == steps - 2:
            gram_ref[...] = jnp.zeros_like(gram_ref)

            def gram_body(row, carry):
                left = wide(row)
                gram_ref[...] += lax.dot_general(left, left, contract, preferred_element_type=jnp.float32)
                return carry

            lax.fori_loop(0, rows, gram_body, 0)

    ritz_ref[...] = jnp.zeros_like(ritz_ref)

    def ritz_body(row, carry):
        right = jnp.concatenate([images[row, col] for col in range(cols)], axis=1)
        ritz_ref[...] += lax.dot_general(wide(row), right, contract, preferred_element_type=jnp.float32)
        return carry

    lax.fori_loop(0, rows, ritz_body, 0)
    for copy in out_copies:
        copy.wait()


def on_device(elem_count, band_count, basis_counts, neighbour_codes, x_block, h_self, h_near):
    rows, cols, columns, basis = x_block.shape
    neighbours = neighbour_codes.shape[2]
    near = h_near.reshape(rows, cols, neighbours * basis, basis)
    ext = pltpu.VMEM((rows + 2, cols + 2, columns // halves, basis), x_block.dtype)
    whole = pl.BlockSpec(memory_space=pltpu.VMEM)
    square = jax.ShapeDtypeStruct((columns, columns), jnp.float32)
    filtered, gram_part, ritz_part = pl.pallas_call(
        functools.partial(kernel, elem_count, band_count),
        out_shape=(jax.ShapeDtypeStruct(x_block.shape, x_block.dtype), square, square),
        in_specs=[pl.BlockSpec(memory_space=pltpu.SMEM)] * 2 + [pl.BlockSpec(memory_space=pl.ANY)] * 3,
        out_specs=(pl.BlockSpec(memory_space=pl.ANY), whole, whole),
        scratch_shapes=[ext] * (steps * halves)
        + [
            pltpu.VMEM((rows, cols, (neighbours + 1) * basis, basis), h_self.dtype),
            pltpu.VMEM((rows, cols, columns, basis), x_block.dtype),
            pltpu.SemaphoreType.DMA((steps, halves, len(directions))),
            pltpu.SemaphoreType.DMA((steps, halves, len(directions))),
            pltpu.SemaphoreType.DMA((halves + 2,)),
            pltpu.SemaphoreType.DMA((halves,)),
        ],
        compiler_params=pltpu.CompilerParams(
            collective_id=0, has_side_effects=True, vmem_limit_bytes=48 * 1024 * 1024
        ),
    )(basis_counts, neighbour_codes, x_block, h_self, near)
    normalizer = jnp.float32(rows * cols * elem_count * band_count * basis / 3.0)
    gram_share, ritz_share = (
        lax.psum_scatter(piece.astype(jnp.bfloat16), "band", scatter_dimension=0, tiled=True).astype(
            jnp.float32
        )
        for piece in (gram_part, ritz_part)
    )
    gram_rows, ritz_rows = lax.psum((gram_share, ritz_share), "elem")
    return (filtered, gram_rows / normalizer, ritz_rows / normalizer)


def solution(mesh):
    in_specs = (
        P("elem", "band"),
        P("elem", "band", None),
        P("elem", "band", None, None),
        P("elem", "band", None, None),
        P("elem", "band", None, None, None),
    )
    out_specs = (P("elem", "band", None, None), P("band", None), P("band", None))
    return jax.shard_map(
        functools.partial(on_device, mesh.shape["elem"], mesh.shape["band"]),
        mesh=mesh,
        in_specs=in_specs,
        out_specs=out_specs,
        check_vma=False,
    )
```

```python
import functools

import jax
import jax.numpy as jnp
from jax import lax
from jax.experimental import pallas as pl
from jax.experimental.pallas import tpu as pltpu
from jax.sharding import PartitionSpec as P

MESH = pl.DeviceIdType.MESH
cheb_center = 0.25
cheb_half = 1.5
steps = 4
halves = 2
directions = [(a, b) for a in (-1, 0, 1) for b in (-1, 0, 1) if (a, b) != (0, 0)]


def edge(shift, count):
    if shift == 0:
        return 1, 1, count
    return (count, 0, 1) if shift > 0 else (1, count + 1, 1)


def digits(count):
    found, stride = [], 1
    while stride < count:
        left = count // stride
        radix = 2 if left % 4 and left % 2 == 0 or stride == 1 and left % 2 == 0 else 4 if left % 4 == 0 else left
        found.append((stride, radix))
        stride *= radix
    return found


def kernel(elem_count, band_count, counts_ref, codes_ref, x_ref, self_ref, near_ref, out_ref, gram_ref, ritz_ref, *scratch):
    exts = [scratch[step * halves : (step + 1) * halves] for step in range(steps)]
    (
        blocks, images, totals, counts, codes, send_sem, recv_sem, load_sem, out_sem,
        outgoing, sum_send, sum_recv, *stage_refs
    ) = scratch[steps * halves :]
    neighbours, cols, rows = codes_ref.shape
    columns, basis = x_ref.shape[2:]
    part = columns // halves
    depth = near_ref.shape[2]
    owned = columns // band_count
    padded = outgoing.shape[2]
    stages = [("band", 1, band_count)] + [("elem", stride, radix) for stride, radix in digits(elem_count)]
    arrived = [stage_refs[m * len(stages) : (m + 1) * len(stages)] for m in range(2)]

    my_elem, my_band = lax.axis_index("elem"), lax.axis_index("band")
    partners = [
        (lax.rem(my_elem + a + elem_count, elem_count), lax.rem(my_band + b + band_count, band_count))
        for a, b in directions
    ]

    small_loads = [
        pltpu.make_async_copy(counts_ref, counts, load_sem.at[halves + 2]),
        pltpu.make_async_copy(codes_ref, codes, load_sem.at[halves + 3]),
    ]
    x_loads = [
        pltpu.make_async_copy(
            x_ref.at[:, :, pl.ds(half * part, part)],
            exts[0][half].at[pl.ds(1, rows), pl.ds(1, cols)],
            load_sem.at[half],
        )
        for half in range(halves)
    ]
    h_loads = [
        pltpu.make_async_copy(near_ref, blocks.at[:, :, pl.ds(0, depth)], load_sem.at[halves]),
        pltpu.make_async_copy(self_ref, blocks.at[:, :, pl.ds(depth, basis)], load_sem.at[halves + 1]),
    ]
    for copy in small_loads + x_loads + h_loads:
        copy.start()

    sum_partners = []
    for axis, stride, radix in stages:
        mine = my_band if axis == "band" else my_elem
        digit = lax.rem(mine // stride, radix)
        peers = []
        for shift in range(1, radix):
            other = lax.rem(digit + shift, radix)
            moved = mine + (other - digit) * stride
            peers.append((other, (my_elem, moved) if axis == "band" else (moved, my_band)))
        sum_partners.append((digit, peers))

    greeted = partners + [device for _, peers in sum_partners for _, device in peers]
    barrier = pltpu.get_barrier_semaphore()
    for partner in greeted:
        pl.semaphore_signal(barrier, inc=1, device_id=partner, device_id_type=MESH)
    pl.semaphore_wait(barrier, len(greeted))
    for copy in small_loads:
        copy.wait()

    lanes = lax.broadcasted_iota(jnp.int32, (part, basis), 1)

    def halo(step, half, which):
        a, b = directions[which]
        row_from, row_to, row_len = edge(a, rows)
        col_from, col_to, col_len = edge(b, cols)
        ext = exts[step][half]
        return pltpu.make_async_remote_copy(
            src_ref=ext.at[pl.ds(row_from, row_len), pl.ds(col_from, col_len)],
            dst_ref=ext.at[pl.ds(row_to, row_len), pl.ds(col_to, col_len)],
            send_sem=send_sem.at[step, half, which],
            recv_sem=recv_sem.at[step, half, which],
            device_id=partners[which],
            device_id_type=MESH,
        )

    vertical = [d for d, (a, b) in enumerate(directions) if a != 0]
    sideways = [d for d, (a, b) in enumerate(directions) if a == 0]

    totals[...] = jnp.zeros_like(totals)
    outgoing[...] = jnp.zeros_like(outgoing)
    for half in range(halves):
        x_loads[half].wait()
        ext = exts[0][half]

        def clear(row, carry, ext=ext):
            for col in range(cols):
                held = ext[row + 1, col + 1]
                ext[row + 1, col + 1] = jnp.where(
                    lanes < counts[col, row], held.astype(jnp.float32), 0.0
                ).astype(held.dtype)
            return carry

        lax.fori_loop(0, rows, clear, 0)
        for which in sideways + vertical:
            halo(0, half, which).start()

    def one_row(step, half, row):
        ext = exts[step][half]
        for col in range(cols):
            pieces = []
            for k in range(neighbours):
                code = codes[k, col, row]
                a = (code * 11) >> 5
                pieces.append(ext[row + a, col + code - 3 * a])
            own = ext[row + 1, col + 1]
            pieces.append(own)
            summed = jnp.dot(
                jnp.concatenate(pieces, axis=1), blocks[row, col], preferred_element_type=jnp.float32
            )
            if step < steps - 1:
                value = (summed - cheb_center * own.astype(jnp.float32)) * (
                    (1.0 if step == 0 else 2.0) / cheb_half
                )
                if step > 0:
                    value = value - exts[step - 1][half][row + 1, col + 1].astype(jnp.float32)
                value = jnp.where(lanes < counts[col, row], value, 0.0)
                exts[step + 1][half][row + 1, col + 1] = value.astype(own.dtype)
            else:
                value = jnp.where(lanes < counts[col, row], summed, 0.0)
                images[row, col, pl.ds(half * part, part)] = value.astype(own.dtype)

    def row_loop(first, count, stride, step, half):
        def body(i, carry):
            one_row(step, half, first + i * stride)
            return carry

        lax.fori_loop(0, count, body, 0)

    def wide(row):
        return jnp.concatenate(
            [
                jnp.concatenate([exts[steps - 1][half][row + 1, col + 1] for half in range(halves)], axis=0)
                for col in range(cols)
            ],
            axis=1,
        )

    def sum_copy(which, stage, shift):
        digit, peers = sum_partners[stage]
        other, device = peers[shift]
        landing = arrived[which][stage].at[digit]
        return pltpu.make_async_remote_copy(
            src_ref=outgoing.at[which, other] if stage == 0 else landing,
            dst_ref=landing,
            send_sem=sum_send.at[which, stage, shift],
            recv_sem=sum_recv.at[which, stage, shift],
            device_id=device,
            device_id_type=MESH,
        )

    def send_stage(which, stage):
        for shift in range(stages[stage][2] - 1):
            sum_copy(which, stage, shift).start()

    def begin_sum(which):
        for block in range(band_count):
            outgoing[which, block, pl.ds(0, owned)] = totals[which, pl.ds(block * owned, owned)].astype(
                outgoing.dtype
            )
        send_stage(which, 0)
        mine = sum_partners[0][0]
        arrived[which][0][mine] = outgoing[which, mine]

    def finish_stage(which, stage):
        for shift in range(stages[stage][2] - 1):
            sum_copy(which, stage, shift).wait()
        ref = arrived[which][stage]
        total = ref[0].astype(jnp.float32)
        for slot in range(1, stages[stage][2]):
            total = total + ref[slot].astype(jnp.float32)
        if stage + 1 < len(stages):
            arrived[which][stage + 1][sum_partners[stage + 1][0]] = total.astype(ref.dtype)
            send_stage(which, stage + 1)
        else:
            scale = 3.0 / (rows * cols * elem_count * band_count * basis)
            (gram_ref, ritz_ref)[which][...] = total[:owned] * scale

    contract = (((1,), (1,)), ((), ()))
    out_copies = []
    for step in range(steps):
        for half in range(halves):
            for which in range(len(directions)):
                halo(step, half, which).wait()
            if step == 0 and half == 0:
                for copy in h_loads:
                    copy.wait()
            row_loop(0, 2, rows - 1, step, half)
            if step < steps - 1:
                for which in vertical:
                    halo(step + 1, half, which).start()
            row_loop(1, rows - 2, 1, step, half)
            if step < steps - 1:
                for which in sideways:
                    halo(step + 1, half, which).start()
            if step == steps - 2:
                out_copies.append(
                    pltpu.make_async_copy(
                        exts[steps - 1][half].at[pl.ds(1, rows), pl.ds(1, cols)],
                        out_ref.at[:, :, pl.ds(half * part, part)],
                        out_sem.at[half],
                    )
                )
                out_copies[-1].start()
            if step == steps - 1 and half < len(stages) - 1:
                finish_stage(0, half)
        if step == steps - 2:

            def gram_body(row, carry):
                left = wide(row)
                totals[0] += lax.dot_general(left, left, contract, preferred_element_type=jnp.float32)
                return carry

            lax.fori_loop(0, rows, gram_body, 0)
            begin_sum(0)

    def ritz_body(row, carry):
        right = jnp.concatenate([images[row, col] for col in range(cols)], axis=1)
        totals[1] += lax.dot_general(wide(row), right, contract, preferred_element_type=jnp.float32)
        return carry

    lax.fori_loop(0, rows, ritz_body, 0)
    begin_sum(1)
    for stage in range(min(halves, len(stages) - 1), len(stages)):
        finish_stage(0, stage)
    for stage in range(len(stages)):
        finish_stage(1, stage)
    for copy in out_copies:
        copy.wait()


def on_device(elem_count, band_count, basis_counts, neighbour_codes, x_block, h_self, h_near):
    rows, cols, columns, basis = x_block.shape
    neighbours = neighbour_codes.shape[2]
    near = h_near.reshape(rows, cols, neighbours * basis, basis)
    ext = pltpu.VMEM((rows + 2, cols + 2, columns // halves, basis), x_block.dtype)
    whole = pl.BlockSpec(memory_space=pltpu.VMEM)
    owned = columns // band_count
    padded = -(-owned // 16) * 16
    share = jax.ShapeDtypeStruct((owned, columns), jnp.float32)
    radices = [band_count] + [radix for _, radix in digits(elem_count)]
    landing = [pltpu.VMEM((radix, padded, columns), jnp.bfloat16) for radix in radices]
    anywhere = pl.BlockSpec(memory_space=pl.ANY)
    return pl.pallas_call(
        functools.partial(kernel, elem_count, band_count),
        out_shape=(jax.ShapeDtypeStruct(x_block.shape, x_block.dtype), share, share),
        in_specs=[anywhere] * 5,
        out_specs=(anywhere, whole, whole),
        scratch_shapes=[ext] * (steps * halves)
        + [
            pltpu.VMEM((rows, cols, (neighbours + 1) * basis, basis), h_self.dtype),
            pltpu.VMEM((rows, cols, columns, basis), x_block.dtype),
            pltpu.VMEM((2, columns, columns), jnp.float32),
            pltpu.SMEM((cols, rows), jnp.int32),
            pltpu.SMEM((neighbours, cols, rows), jnp.int32),
            pltpu.SemaphoreType.DMA((steps, halves, len(directions))),
            pltpu.SemaphoreType.DMA((steps, halves, len(directions))),
            pltpu.SemaphoreType.DMA((halves + 4,)),
            pltpu.SemaphoreType.DMA((halves,)),
            pltpu.VMEM((2, band_count, padded, columns), jnp.bfloat16),
            pltpu.SemaphoreType.DMA((2, len(radices), max(radices) - 1)),
            pltpu.SemaphoreType.DMA((2, len(radices), max(radices) - 1)),
        ]
        + landing * 2,
        compiler_params=pltpu.CompilerParams(
            collective_id=0, has_side_effects=True, vmem_limit_bytes=60 * 1024 * 1024
        ),
    )(basis_counts.T, neighbour_codes.transpose(2, 1, 0), x_block, h_self, near)


def solution(mesh):
    in_specs = (
        P("elem", "band"),
        P("elem", "band", None),
        P("elem", "band", None, None),
        P("elem", "band", None, None),
        P("elem", "band", None, None, None),
    )
    out_specs = (P("elem", "band", None, None), P("band", None), P("band", None))
    return jax.shard_map(
        functools.partial(on_device, mesh.shape["elem"], mesh.shape["band"]),
        mesh=mesh,
        in_specs=in_specs,
        out_specs=out_specs,
        check_vma=False,
    )
```

```python
import functools

import jax
import jax.numpy as jnp
from jax import lax
from jax.experimental import pallas as pl
from jax.experimental.pallas import tpu as pltpu
from jax.sharding import PartitionSpec as P

MESH = pl.DeviceIdType.MESH
cheb_center = 0.25
cheb_half = 1.5
steps = 4
halves = 2
ways = ("vertical", "far", "near", "sideways")


def edge(shift, count):
    if shift == 0:
        return 1, 1, count
    return (count, 0, 1) if shift > 0 else (1, count + 1, 1)


def digits(count):
    found, stride = [], 1
    while stride < count:
        left = count // stride
        radix = 2 if left % 4 and left % 2 == 0 or stride == 1 and left % 2 == 0 else 4 if left % 4 == 0 else left
        found.append((stride, radix))
        stride *= radix
    return found


def kernel(elem_count, band_count, counts_ref, codes_ref, x_ref, self_ref, near_ref, out_ref, gram_ref, ritz_ref, *scratch):
    exts = [scratch[step * halves : (step + 1) * halves] for step in range(steps)]
    (
        blocks, totals, counts, codes, send_sem, recv_sem, load_sem, out_sem,
        outgoing, sum_send, sum_recv, *stage_refs
    ) = scratch[steps * halves :]
    neighbours, cols, rows = codes_ref.shape
    columns, basis = x_ref.shape[2:]
    part = columns // halves
    depth = near_ref.shape[2]
    owned = columns // band_count
    padded = outgoing.shape[2]
    stages = [("band", 1, band_count)] + [("elem", stride, radix) for stride, radix in digits(elem_count)]
    arrived = [stage_refs[m * len(stages) : (m + 1) * len(stages)] for m in range(2 * halves)]

    my_elem, my_band = lax.axis_index("elem"), lax.axis_index("band")
    odd = lax.rem(my_band, 2)
    inward, outward = 1 - 2 * odd, 2 * odd - 1
    moves = [(way, shift) for way in ways for shift in (-1, 1)]

    def device_at(a, b):
        return lax.rem(my_elem + a + elem_count, elem_count), lax.rem(my_band + b + band_count, band_count)

    partners = [device_at(a, b) for a in (-1, 0, 1) for b in (-1, 0, 1) if (a, b) != (0, 0)]

    small_loads = [
        pltpu.make_async_copy(counts_ref, counts, load_sem.at[halves + 2]),
        pltpu.make_async_copy(codes_ref, codes, load_sem.at[halves + 3]),
    ]
    x_loads = [
        pltpu.make_async_copy(
            x_ref.at[:, :, pl.ds(half * part, part)],
            exts[0][half].at[pl.ds(1, rows), pl.ds(1, cols)],
            load_sem.at[half],
        )
        for half in range(halves)
    ]
    h_loads = [
        pltpu.make_async_copy(near_ref, blocks.at[:, :, pl.ds(0, depth)], load_sem.at[halves]),
        pltpu.make_async_copy(self_ref, blocks.at[:, :, pl.ds(depth, basis)], load_sem.at[halves + 1]),
    ]
    for copy in small_loads + x_loads + h_loads:
        copy.start()

    sum_partners = []
    for axis, stride, radix in stages:
        mine = my_band if axis == "band" else my_elem
        digit = lax.rem(mine // stride, radix)
        peers = []
        for shift in range(1, radix):
            other = lax.rem(digit + shift, radix)
            moved = mine + (other - digit) * stride
            peers.append((other, (my_elem, moved) if axis == "band" else (moved, my_band)))
        sum_partners.append((digit, peers))

    greeted = partners + [device for _, peers in sum_partners for _, device in peers]
    barrier = pltpu.get_barrier_semaphore()
    for partner in greeted:
        pl.semaphore_signal(barrier, inc=1, device_id=partner, device_id_type=MESH)
    pl.semaphore_wait(barrier, len(greeted))
    for copy in small_loads:
        copy.wait()

    lanes = lax.broadcasted_iota(jnp.int32, (part, basis), 1)

    def halo(step, half, which):
        way, shift = moves[which]
        ext = exts[step][half]
        if way == "vertical":
            start, landing, length = edge(shift, rows)
            src = ext.at[pl.ds(start, length), pl.ds(1, cols)]
            dst = ext.at[pl.ds(landing, length), pl.ds(1, cols)]
            device = device_at(shift, 0)
        elif way == "sideways":
            start, landing, length = edge(shift, cols)
            src = ext.at[pl.ds(1, rows), pl.ds(start, length)]
            dst = ext.at[pl.ds(1, rows), pl.ds(landing, length)]
            device = device_at(0, shift)
        elif way == "far":
            start, landing, length = edge(shift, rows)
            src = ext.at[pl.ds(start, length), pl.ds(1 + odd * (cols - 1), 1)]
            dst = ext.at[pl.ds(landing, length), pl.ds((1 - odd) * (cols + 1), 1)]
            device = device_at(shift, outward)
        else:
            row = 0 if shift < 0 else rows + 1
            src = ext.at[pl.ds(row, 1), pl.ds(cols - odd * (cols - 1), 1)]
            dst = ext.at[pl.ds(row, 1), pl.ds(odd * (cols + 1), 1)]
            device = device_at(0, inward)
        return pltpu.make_async_remote_copy(
            src_ref=src,
            dst_ref=dst,
            send_sem=send_sem.at[step, half, which],
            recv_sem=recv_sem.at[step, half, which],
            device_id=device,
            device_id_type=MESH,
        )

    def chosen(*wanted):
        return [index for index, (way, shift) in enumerate(moves) if way in wanted]

    totals[...] = jnp.zeros_like(totals)
    outgoing[...] = jnp.zeros_like(outgoing)
    for half in range(halves):
        x_loads[half].wait()
        ext = exts[0][half]

        def clear(row, carry, ext=ext):
            for col in range(cols):
                held = ext[row + 1, col + 1]
                ext[row + 1, col + 1] = jnp.where(
                    lanes < counts[col, row], held.astype(jnp.float32), 0.0
                ).astype(held.dtype)
            return carry

        lax.fori_loop(0, rows, clear, 0)
        for which in chosen("vertical", "far", "sideways"):
            halo(0, half, which).start()

    contract = (((1,), (1,)), ((), ()))

    def wide(row):
        return jnp.concatenate(
            [
                jnp.concatenate([exts[steps - 1][half][row + 1, col + 1] for half in range(halves)], axis=0)
                for col in range(cols)
            ],
            axis=1,
        )

    def one_row(step, half, row):
        ext = exts[step][half]
        images = []
        for col in range(cols):
            pieces = []
            for k in range(neighbours):
                code = codes[k, col, row]
                a = (code * 11) >> 5
                pieces.append(ext[row + a, col + code - 3 * a])
            own = ext[row + 1, col + 1]
            pieces.append(own)
            summed = jnp.dot(
                jnp.concatenate(pieces, axis=1), blocks[row, col], preferred_element_type=jnp.float32
            )
            if step < steps - 1:
                value = (summed - cheb_center * own.astype(jnp.float32)) * (
                    (1.0 if step == 0 else 2.0) / cheb_half
                )
                if step > 0:
                    value = value - exts[step - 1][half][row + 1, col + 1].astype(jnp.float32)
                value = jnp.where(lanes < counts[col, row], value, 0.0)
                exts[step + 1][half][row + 1, col + 1] = value.astype(own.dtype)
            else:
                value = jnp.where(lanes < counts[col, row], summed, 0.0)
                images.append(value.astype(own.dtype))
        if images:
            totals[halves + half] += lax.dot_general(
                wide(row), jnp.concatenate(images, axis=1), contract, preferred_element_type=jnp.float32
            )

    def row_loop(first, count, stride, step, half):
        def body(i, carry):
            one_row(step, half, first + i * stride)
            return carry

        lax.fori_loop(0, count, body, 0)

    def sum_copy(which, stage, shift):
        digit, peers = sum_partners[stage]
        other, device = peers[shift]
        landing = arrived[which][stage].at[digit]
        return pltpu.make_async_remote_copy(
            src_ref=outgoing.at[which, other] if stage == 0 else landing,
            dst_ref=landing,
            send_sem=sum_send.at[which, stage, shift],
            recv_sem=sum_recv.at[which, stage, shift],
            device_id=device,
            device_id_type=MESH,
        )

    def send_stage(which, stage):
        for shift in range(stages[stage][2] - 1):
            sum_copy(which, stage, shift).start()

    def begin_sum(which):
        for block in range(band_count):
            outgoing[which, block, pl.ds(0, owned)] = totals[which, pl.ds(block * owned, owned)].astype(
                outgoing.dtype
            )
        send_stage(which, 0)
        mine = sum_partners[0][0]
        arrived[which][0][mine] = outgoing[which, mine]

    def finish_stage(which, stage):
        for shift in range(stages[stage][2] - 1):
            sum_copy(which, stage, shift).wait()
        ref = arrived[which][stage]
        total = ref[0].astype(jnp.float32)
        for slot in range(1, stages[stage][2]):
            total = total + ref[slot].astype(jnp.float32)
        if stage + 1 < len(stages):
            arrived[which][stage + 1][sum_partners[stage + 1][0]] = total.astype(ref.dtype)
            send_stage(which, stage + 1)
        else:
            scale = 3.0 / (rows * cols * elem_count * band_count * basis)
            (gram_ref, ritz_ref)[which // halves][:, pl.ds(which % halves * part, part)] = total[:owned] * scale

    contract = (((1,), (1,)), ((), ()))
    out_copies = []
    for step in range(steps):
        for half in range(halves):
            for which in chosen("vertical"):
                halo(step, half, which).wait()
            for which in chosen("near"):
                halo(step, half, which).start()
            for which in chosen("far", "sideways", "near"):
                halo(step, half, which).wait()
            if step == 0 and half == 0:
                for copy in h_loads:
                    copy.wait()
            row_loop(0, 2, rows - 1, step, half)
            if step < steps - 1:
                for which in chosen("vertical", "far"):
                    halo(step + 1, half, which).start()
            row_loop(1, rows - 2, 1, step, half)
            if step < steps - 1:
                for which in chosen("sideways"):
                    halo(step + 1, half, which).start()
            if step == steps - 2:
                out_copies.append(
                    pltpu.make_async_copy(
                        exts[steps - 1][half].at[pl.ds(1, rows), pl.ds(1, cols)],
                        out_ref.at[:, :, pl.ds(half * part, part)],
                        out_sem.at[half],
                    )
                )
                out_copies[-1].start()
            if step == steps - 1:
                begin_sum(halves + half)
                if half < len(stages) - 1:
                    for which in range(halves):
                        finish_stage(which, half)
        if step == steps - 2:

            def gram_body(row, carry):
                left = wide(row)
                for half in range(halves):
                    right = left[half * part : (half + 1) * part]
                    totals[half] += lax.dot_general(left, right, contract, preferred_element_type=jnp.float32)
                return carry

            lax.fori_loop(0, rows, gram_body, 0)
            for half in range(halves):
                begin_sum(half)

    for stage in range(len(stages)):
        for which in range(2 * halves):
            if which >= halves or stage >= min(halves, len(stages) - 1):
                finish_stage(which, stage)
    for copy in out_copies:
        copy.wait()


def on_device(elem_count, band_count, basis_counts, neighbour_codes, x_block, h_self, h_near):
    rows, cols, columns, basis = x_block.shape
    neighbours = neighbour_codes.shape[2]
    near = h_near.reshape(rows, cols, neighbours * basis, basis)
    ext = pltpu.VMEM((rows + 2, cols + 2, columns // halves, basis), x_block.dtype)
    whole = pl.BlockSpec(memory_space=pltpu.VMEM)
    owned = columns // band_count
    padded = -(-owned // 16) * 16
    share = jax.ShapeDtypeStruct((owned, columns), jnp.float32)
    radices = [band_count] + [radix for _, radix in digits(elem_count)]
    landing = [pltpu.VMEM((radix, padded, columns // halves), jnp.bfloat16) for radix in radices]
    anywhere = pl.BlockSpec(memory_space=pl.ANY)
    return pl.pallas_call(
        functools.partial(kernel, elem_count, band_count),
        out_shape=(jax.ShapeDtypeStruct(x_block.shape, x_block.dtype), share, share),
        in_specs=[anywhere] * 5,
        out_specs=(anywhere, whole, whole),
        scratch_shapes=[ext] * (steps * halves)
        + [
            pltpu.VMEM((rows, cols, (neighbours + 1) * basis, basis), h_self.dtype),
            pltpu.VMEM((2 * halves, columns, columns // halves), jnp.float32),
            pltpu.SMEM((cols, rows), jnp.int32),
            pltpu.SMEM((neighbours, cols, rows), jnp.int32),
            pltpu.SemaphoreType.DMA((steps, halves, 2 * len(ways))),
            pltpu.SemaphoreType.DMA((steps, halves, 2 * len(ways))),
            pltpu.SemaphoreType.DMA((halves + 4,)),
            pltpu.SemaphoreType.DMA((halves,)),
            pltpu.VMEM((2 * halves, band_count, padded, columns // halves), jnp.bfloat16),
            pltpu.SemaphoreType.DMA((2 * halves, len(radices), max(radices) - 1)),
            pltpu.SemaphoreType.DMA((2 * halves, len(radices), max(radices) - 1)),
        ]
        + landing * (2 * halves),
        compiler_params=pltpu.CompilerParams(
            collective_id=0, has_side_effects=True, vmem_limit_bytes=60 * 1024 * 1024
        ),
    )(basis_counts.T, neighbour_codes.transpose(2, 1, 0), x_block, h_self, near)


def solution(mesh):
    in_specs = (
        P("elem", "band"),
        P("elem", "band", None),
        P("elem", "band", None, None),
        P("elem", "band", None, None),
        P("elem", "band", None, None, None),
    )
    out_specs = (P("elem", "band", None, None), P("band", None), P("band", None))
    return jax.shard_map(
        functools.partial(on_device, mesh.shape["elem"], mesh.shape["band"]),
        mesh=mesh,
        in_specs=in_specs,
        out_specs=out_specs,
        check_vma=False,
    )
```

```python
import functools

import jax
import jax.numpy as jnp
from jax import lax
from jax.experimental import pallas as pl
from jax.experimental.pallas import tpu as pltpu
from jax.sharding import PartitionSpec as P

MESH = pl.DeviceIdType.MESH
cheb_center = 0.25
cheb_half = 1.5
steps = 4
halves = 2
ways = ("vertical", "far", "near", "sideways")


def edge(shift, count):
    if shift == 0:
        return 1, 1, count
    return (count, 0, 1) if shift > 0 else (1, count + 1, 1)


def digits(count):
    found, stride = [], 1
    while stride < count:
        left = count // stride
        radix = 2 if left % 4 and left % 2 == 0 or stride == 1 and left % 2 == 0 else 4 if left % 4 == 0 else left
        found.append((stride, radix))
        stride *= radix
    return found


def kernel(elem_count, band_count, counts_ref, codes_ref, x_ref, self_ref, near_ref, out_ref, gram_ref, ritz_ref, *scratch):
    exts = [scratch[step * halves : (step + 1) * halves] for step in range(steps)]
    (
        blocks, images, totals, counts, codes, send_sem, recv_sem, load_sem, out_sem,
        outgoing, sum_send, sum_recv, *stage_refs
    ) = scratch[steps * halves :]
    neighbours, cols, rows = codes_ref.shape
    columns, basis = x_ref.shape[2:]
    part = columns // halves
    depth = near_ref.shape[2]
    owned = columns // band_count
    padded = outgoing.shape[2]
    stages = [("band", 1, band_count)] + [("elem", stride, radix) for stride, radix in digits(elem_count)]
    arrived = [stage_refs[m * len(stages) : (m + 1) * len(stages)] for m in range(2 * halves)]

    my_elem, my_band = lax.axis_index("elem"), lax.axis_index("band")
    odd = lax.rem(my_band, 2)
    inward, outward = 1 - 2 * odd, 2 * odd - 1
    moves = [(way, shift) for way in ways for shift in (-1, 1)]

    def device_at(a, b):
        return lax.rem(my_elem + a + elem_count, elem_count), lax.rem(my_band + b + band_count, band_count)

    partners = [device_at(a, b) for a in (-1, 0, 1) for b in (-1, 0, 1) if (a, b) != (0, 0)]

    small_loads = [
        pltpu.make_async_copy(counts_ref, counts, load_sem.at[halves + 2]),
        pltpu.make_async_copy(codes_ref, codes, load_sem.at[halves + 3]),
    ]
    x_loads = [
        pltpu.make_async_copy(
            x_ref.at[:, :, pl.ds(half * part, part)],
            exts[0][half].at[pl.ds(1, rows), pl.ds(1, cols)],
            load_sem.at[half],
        )
        for half in range(halves)
    ]
    h_loads = [
        pltpu.make_async_copy(near_ref, blocks.at[:, :, pl.ds(0, depth)], load_sem.at[halves]),
        pltpu.make_async_copy(self_ref, blocks.at[:, :, pl.ds(depth, basis)], load_sem.at[halves + 1]),
    ]
    for copy in small_loads + x_loads + h_loads:
        copy.start()

    sum_partners = []
    for axis, stride, radix in stages:
        mine = my_band if axis == "band" else my_elem
        digit = lax.rem(mine // stride, radix)
        peers = []
        for shift in range(1, radix):
            other = lax.rem(digit + shift, radix)
            moved = mine + (other - digit) * stride
            peers.append((other, (my_elem, moved) if axis == "band" else (moved, my_band)))
        sum_partners.append((digit, peers))

    greeted = partners + [device for _, peers in sum_partners for _, device in peers]
    barrier = pltpu.get_barrier_semaphore()
    for partner in greeted:
        pl.semaphore_signal(barrier, inc=1, device_id=partner, device_id_type=MESH)
    pl.semaphore_wait(barrier, len(greeted))
    for copy in small_loads:
        copy.wait()

    lanes = lax.broadcasted_iota(jnp.int32, (part, basis), 1)

    def halo(step, half, which):
        way, shift = moves[which]
        ext = exts[step][half]
        if way == "vertical":
            start, landing, length = edge(shift, rows)
            src = ext.at[pl.ds(start, length), pl.ds(1, cols)]
            dst = ext.at[pl.ds(landing, length), pl.ds(1, cols)]
            device = device_at(shift, 0)
        elif way == "sideways":
            start, landing, length = edge(shift, cols)
            src = ext.at[pl.ds(1, rows), pl.ds(start, length)]
            dst = ext.at[pl.ds(1, rows), pl.ds(landing, length)]
            device = device_at(0, shift)
        elif way == "far":
            start, landing, length = edge(shift, rows)
            src = ext.at[pl.ds(start, length), pl.ds(1 + odd * (cols - 1), 1)]
            dst = ext.at[pl.ds(landing, length), pl.ds((1 - odd) * (cols + 1), 1)]
            device = device_at(shift, outward)
        else:
            row = 0 if shift < 0 else rows + 1
            src = ext.at[pl.ds(row, 1), pl.ds(cols - odd * (cols - 1), 1)]
            dst = ext.at[pl.ds(row, 1), pl.ds(odd * (cols + 1), 1)]
            device = device_at(0, inward)
        return pltpu.make_async_remote_copy(
            src_ref=src,
            dst_ref=dst,
            send_sem=send_sem.at[step, half, which],
            recv_sem=recv_sem.at[step, half, which],
            device_id=device,
            device_id_type=MESH,
        )

    def chosen(*wanted):
        return [index for index, (way, shift) in enumerate(moves) if way in wanted]

    totals[...] = jnp.zeros_like(totals)
    outgoing[...] = jnp.zeros_like(outgoing)
    for half in range(halves):
        x_loads[half].wait()
        ext = exts[0][half]

        def clear(row, carry, ext=ext):
            for col in range(cols):
                held = ext[row + 1, col + 1]
                ext[row + 1, col + 1] = jnp.where(
                    lanes < counts[col, row], held.astype(jnp.float32), 0.0
                ).astype(held.dtype)
            return carry

        lax.fori_loop(0, rows, clear, 0)
        for which in chosen("vertical", "far", "sideways"):
            halo(0, half, which).start()

    contract = (((1,), (1,)), ((), ()))

    def wide(row):
        return jnp.concatenate(
            [
                jnp.concatenate([exts[steps - 1][half][row + 1, col + 1] for half in range(halves)], axis=0)
                for col in range(cols)
            ],
            axis=1,
        )

    def update(step, half, places):
        ext = exts[step][half]
        for row, col in places:
            pieces = []
            for k in range(neighbours):
                code = codes[k, col, row]
                a = (code * 11) >> 5
                pieces.append(ext[row + a, col + code - 3 * a])
            own = ext[row + 1, col + 1]
            pieces.append(own)
            summed = jnp.dot(
                jnp.concatenate(pieces, axis=1), blocks[row, col], preferred_element_type=jnp.float32
            )
            if step < steps - 1:
                value = (summed - cheb_center * own.astype(jnp.float32)) * (
                    (1.0 if step == 0 else 2.0) / cheb_half
                )
                if step > 0:
                    value = value - exts[step - 1][half][row + 1, col + 1].astype(jnp.float32)
                value = jnp.where(lanes < counts[col, row], value, 0.0)
                exts[step + 1][half][row + 1, col + 1] = value.astype(own.dtype)
            else:
                value = jnp.where(lanes < counts[col, row], summed, 0.0)
                images[row, col] = value.astype(own.dtype)

    def loop(count, body):
        def run(index, carry):
            body(index)
            return carry

        lax.fori_loop(0, count, run, 0)

    group = 2 if rows % 2 == 0 else 1

    def inner(step, half, wanted):
        def body(index):
            update(step, half, [(1 + index * group + i, col) for i in range(group) for col in wanted])

        loop((rows - 2) // group, body)

    def add_ritz(half):
        def body(row):
            right = jnp.concatenate([images[row, col] for col in range(cols)], axis=1)
            totals[halves + half] += lax.dot_general(wide(row), right, contract, preferred_element_type=jnp.float32)

        loop(rows, body)

    def sum_copy(which, stage, shift):
        digit, peers = sum_partners[stage]
        other, device = peers[shift]
        landing = arrived[which][stage].at[digit]
        return pltpu.make_async_remote_copy(
            src_ref=outgoing.at[which, other] if stage == 0 else landing,
            dst_ref=landing,
            send_sem=sum_send.at[which, stage, shift],
            recv_sem=sum_recv.at[which, stage, shift],
            device_id=device,
            device_id_type=MESH,
        )

    def send_stage(which, stage):
        for shift in range(stages[stage][2] - 1):
            sum_copy(which, stage, shift).start()

    def begin_sum(which):
        for block in range(band_count):
            outgoing[which, block, pl.ds(0, owned)] = totals[which, pl.ds(block * owned, owned)].astype(
                outgoing.dtype
            )
        send_stage(which, 0)
        mine = sum_partners[0][0]
        arrived[which][0][mine] = outgoing[which, mine]

    def finish_stage(which, stage):
        for shift in range(stages[stage][2] - 1):
            sum_copy(which, stage, shift).wait()
        ref = arrived[which][stage]
        total = ref[0].astype(jnp.float32)
        for slot in range(1, stages[stage][2]):
            total = total + ref[slot].astype(jnp.float32)
        if stage + 1 < len(stages):
            arrived[which][stage + 1][sum_partners[stage + 1][0]] = total.astype(ref.dtype)
            send_stage(which, stage + 1)
        else:
            scale = 3.0 / (rows * cols * elem_count * band_count * basis)
            (gram_ref, ritz_ref)[which // halves][:, pl.ds(which % halves * part, part)] = total[:owned] * scale

    out_copies = []
    for step in range(steps):
        for half in range(halves):
            for which in chosen("vertical"):
                halo(step, half, which).wait()
            for which in chosen("near"):
                halo(step, half, which).start()
            for which in chosen("far", "sideways", "near"):
                halo(step, half, which).wait()
            if step == 0 and half == 0:
                for copy in h_loads:
                    copy.wait()
            update(step, half, [(row, col) for row in (0, rows - 1) for col in range(cols)])
            if step < steps - 1:
                for which in chosen("vertical", "far"):
                    halo(step + 1, half, which).start()
            inner(step, half, (0, cols - 1))
            if step < steps - 1:
                for which in chosen("sideways"):
                    halo(step + 1, half, which).start()
            inner(step, half, range(1, cols - 1))
            if step == steps - 2:
                out_copies.append(
                    pltpu.make_async_copy(
                        exts[steps - 1][half].at[pl.ds(1, rows), pl.ds(1, cols)],
                        out_ref.at[:, :, pl.ds(half * part, part)],
                        out_sem.at[half],
                    )
                )
                out_copies[-1].start()
            if step == steps - 1:
                add_ritz(half)
                begin_sum(halves + half)
                if half < len(stages) - 1:
                    for which in range(halves):
                        finish_stage(which, half)
        if step == steps - 2:

            def gram_body(row, carry):
                left = wide(row)
                for half in range(halves):
                    right = left[half * part : (half + 1) * part]
                    totals[half] += lax.dot_general(left, right, contract, preferred_element_type=jnp.float32)
                return carry

            lax.fori_loop(0, rows, gram_body, 0)
            for half in range(halves):
                begin_sum(half)

    for stage in range(len(stages)):
        for which in range(2 * halves):
            if which >= halves or stage >= min(halves, len(stages) - 1):
                finish_stage(which, stage)
    for copy in out_copies:
        copy.wait()


def hand_on(*refs):
    count = len(refs) // 2
    copies = []
    for index, (source, target) in enumerate(zip(refs[:count], refs[count:-1])):
        if len(source.shape) == 2:
            copies.append((source, target))
        else:
            copies.extend((source.at[row], target.at[row]) for row in range(source.shape[0]))
    started = [pltpu.make_async_copy(*pair, refs[-1].at[i]) for i, pair in enumerate(copies)]
    for copy in started:
        copy.start()
    for copy in started:
        copy.wait()


def on_device(elem_count, band_count, basis_counts, neighbour_codes, x_block, h_self, h_near):
    rows, cols, columns, basis = x_block.shape
    neighbours = neighbour_codes.shape[2]
    near = h_near.reshape(rows, cols, neighbours * basis, basis)
    ext = pltpu.VMEM((rows + 2, cols + 2, columns // halves, basis), x_block.dtype)
    whole = pl.BlockSpec(memory_space=pltpu.VMEM)
    owned = columns // band_count
    padded = -(-owned // 16) * 16
    share = jax.ShapeDtypeStruct((owned, columns), jnp.float32)
    radices = [band_count] + [radix for _, radix in digits(elem_count)]
    landing = [pltpu.VMEM((radix, padded, columns // halves), jnp.bfloat16) for radix in radices]
    anywhere = pl.BlockSpec(memory_space=pl.ANY)
    results = pl.pallas_call(
        functools.partial(kernel, elem_count, band_count),
        out_shape=(jax.ShapeDtypeStruct(x_block.shape, x_block.dtype), share, share),
        in_specs=[anywhere] * 5,
        out_specs=(anywhere, whole, whole),
        scratch_shapes=[ext] * (steps * halves)
        + [
            pltpu.VMEM((rows, cols, (neighbours + 1) * basis, basis), h_self.dtype),
            pltpu.VMEM((rows, cols, columns // halves, basis), x_block.dtype),
            pltpu.VMEM((2 * halves, columns, columns // halves), jnp.float32),
            pltpu.SMEM((cols, rows), jnp.int32),
            pltpu.SMEM((neighbours, cols, rows), jnp.int32),
            pltpu.SemaphoreType.DMA((steps, halves, 2 * len(ways))),
            pltpu.SemaphoreType.DMA((steps, halves, 2 * len(ways))),
            pltpu.SemaphoreType.DMA((halves + 4,)),
            pltpu.SemaphoreType.DMA((halves,)),
            pltpu.VMEM((2 * halves, band_count, padded, columns // halves), jnp.bfloat16),
            pltpu.SemaphoreType.DMA((2 * halves, len(radices), max(radices) - 1)),
            pltpu.SemaphoreType.DMA((2 * halves, len(radices), max(radices) - 1)),
        ]
        + landing * (2 * halves),
        compiler_params=pltpu.CompilerParams(
            collective_id=0, has_side_effects=True, vmem_limit_bytes=60 * 1024 * 1024
        ),
    )(basis_counts.T, neighbour_codes.transpose(2, 1, 0), x_block, h_self, near)
    return pl.pallas_call(
        hand_on,
        out_shape=tuple(jax.ShapeDtypeStruct(result.shape, result.dtype) for result in results),
        in_specs=[anywhere] * len(results),
        out_specs=(anywhere,) * len(results),
        scratch_shapes=[pltpu.SemaphoreType.DMA((rows + 2,))],
        compiler_params=pltpu.CompilerParams(vmem_limit_bytes=60 * 1024 * 1024),
    )(*results)


def solution(mesh):
    in_specs = (
        P("elem", "band"),
        P("elem", "band", None),
        P("elem", "band", None, None),
        P("elem", "band", None, None),
        P("elem", "band", None, None, None),
    )
    out_specs = (P("elem", "band", None, None), P("band", None), P("band", None))
    return jax.shard_map(
        functools.partial(on_device, mesh.shape["elem"], mesh.shape["band"]),
        mesh=mesh,
        in_specs=in_specs,
        out_specs=out_specs,
        check_vma=False,
    )
```

```python
import functools

import jax
import jax.numpy as jnp
from jax import lax
from jax.experimental import pallas as pl
from jax.experimental.pallas import tpu as pltpu
from jax.sharding import PartitionSpec as P

MESH = pl.DeviceIdType.MESH
cheb_center = 0.25
cheb_half = 1.5
steps = 4
halves = 2
ways = ("vertical", "far", "near", "sideways")


def edge(shift, count):
    if shift == 0:
        return 1, 1, count
    return (count, 0, 1) if shift > 0 else (1, count + 1, 1)


def digits(count):
    found, stride = [], 1
    while stride < count:
        left = count // stride
        radix = 2 if left % 4 and left % 2 == 0 or stride == 1 and left % 2 == 0 else 4 if left % 4 == 0 else left
        found.append((stride, radix))
        stride *= radix
    return found


def kernel(elem_count, band_count, counts_ref, codes_ref, x_ref, self_ref, near_ref, out_ref, gram_ref, ritz_ref, *scratch):
    exts = [scratch[step * halves : (step + 1) * halves] for step in range(steps)]
    (
        blocks, images, totals, counts, codes, send_sem, recv_sem, load_sem, out_sem,
        outgoing, sum_send, sum_recv, *stage_refs
    ) = scratch[steps * halves :]
    neighbours, cols, rows = codes_ref.shape
    columns, basis = x_ref.shape[2:]
    part = columns // halves
    depth = near_ref.shape[2]
    owned = columns // band_count
    padded = outgoing.shape[2]
    stages = [("band", 1, band_count)] + [("elem", stride, radix) for stride, radix in digits(elem_count)]
    arrived = [stage_refs[m * len(stages) : (m + 1) * len(stages)] for m in range(2 * halves)]

    my_elem, my_band = lax.axis_index("elem"), lax.axis_index("band")
    odd = lax.rem(my_band, 2)
    inward, outward = 1 - 2 * odd, 2 * odd - 1
    moves = [(way, shift) for way in ways for shift in (-1, 1)]

    def device_at(a, b):
        return lax.rem(my_elem + a + elem_count, elem_count), lax.rem(my_band + b + band_count, band_count)

    partners = [device_at(a, b) for a in (-1, 0, 1) for b in (-1, 0, 1) if (a, b) != (0, 0)]

    small_loads = [
        pltpu.make_async_copy(counts_ref, counts, load_sem.at[halves + 2]),
        pltpu.make_async_copy(codes_ref, codes, load_sem.at[halves + 3]),
    ]
    x_loads = [
        pltpu.make_async_copy(
            x_ref.at[:, :, pl.ds(half * part, part)],
            exts[0][half].at[pl.ds(1, rows), pl.ds(1, cols)],
            load_sem.at[half],
        )
        for half in range(halves)
    ]
    h_loads = [
        pltpu.make_async_copy(near_ref, blocks.at[:, :, pl.ds(0, depth)], load_sem.at[halves]),
        pltpu.make_async_copy(self_ref, blocks.at[:, :, pl.ds(depth, basis)], load_sem.at[halves + 1]),
    ]
    for copy in small_loads + x_loads + h_loads:
        copy.start()

    sum_partners = []
    for axis, stride, radix in stages:
        mine = my_band if axis == "band" else my_elem
        digit = lax.rem(mine // stride, radix)
        peers = []
        for shift in range(1, radix):
            other = lax.rem(digit + shift, radix)
            moved = mine + (other - digit) * stride
            peers.append((other, (my_elem, moved) if axis == "band" else (moved, my_band)))
        sum_partners.append((digit, peers))

    greeted = partners + [device for _, peers in sum_partners for _, device in peers]
    barrier = pltpu.get_barrier_semaphore()
    for partner in greeted:
        pl.semaphore_signal(barrier, inc=1, device_id=partner, device_id_type=MESH)
    pl.semaphore_wait(barrier, len(greeted))
    for copy in small_loads:
        copy.wait()

    lanes = lax.broadcasted_iota(jnp.int32, (part, basis), 1)

    def halo(step, half, which):
        way, shift = moves[which]
        ext = exts[step][half]
        if way == "vertical":
            start, landing, length = edge(shift, rows)
            src = ext.at[pl.ds(start, length), pl.ds(1, cols)]
            dst = ext.at[pl.ds(landing, length), pl.ds(1, cols)]
            device = device_at(shift, 0)
        elif way == "sideways":
            start, landing, length = edge(shift, cols)
            src = ext.at[pl.ds(1, rows), pl.ds(start, length)]
            dst = ext.at[pl.ds(1, rows), pl.ds(landing, length)]
            device = device_at(0, shift)
        elif way == "far":
            start, landing, length = edge(shift, rows)
            src = ext.at[pl.ds(start, length), pl.ds(1 + odd * (cols - 1), 1)]
            dst = ext.at[pl.ds(landing, length), pl.ds((1 - odd) * (cols + 1), 1)]
            device = device_at(shift, outward)
        else:
            row = 0 if shift < 0 else rows + 1
            src = ext.at[pl.ds(row, 1), pl.ds(cols - odd * (cols - 1), 1)]
            dst = ext.at[pl.ds(row, 1), pl.ds(odd * (cols + 1), 1)]
            device = device_at(0, inward)
        return pltpu.make_async_remote_copy(
            src_ref=src,
            dst_ref=dst,
            send_sem=send_sem.at[step, half, which],
            recv_sem=recv_sem.at[step, half, which],
            device_id=device,
            device_id_type=MESH,
        )

    def chosen(*wanted):
        return [index for index, (way, shift) in enumerate(moves) if way in wanted]

    totals[...] = jnp.zeros_like(totals)
    outgoing[...] = jnp.zeros_like(outgoing)
    for half in range(halves):
        x_loads[half].wait()
        ext = exts[0][half]

        def clear(row, carry, ext=ext):
            for col in range(cols):
                held = ext[row + 1, col + 1]
                ext[row + 1, col + 1] = jnp.where(
                    lanes < counts[col, row], held.astype(jnp.float32), 0.0
                ).astype(held.dtype)
            return carry

        lax.fori_loop(0, rows, clear, 0)
        for which in chosen("vertical", "far", "sideways"):
            halo(0, half, which).start()

    contract = (((1,), (1,)), ((), ()))

    def wide(row):
        return jnp.concatenate(
            [
                jnp.concatenate([exts[steps - 1][half][row + 1, col + 1] for half in range(halves)], axis=0)
                for col in range(cols)
            ],
            axis=1,
        )

    def update(step, half, places):
        ext = exts[step][half]
        made = []
        for row, col in places:
            pieces = []
            for k in range(neighbours):
                code = codes[k, col, row]
                a = (code * 11) >> 5
                pieces.append(ext[row + a, col + code - 3 * a])
            own = ext[row + 1, col + 1]
            pieces.append(own)
            summed = jnp.dot(
                jnp.concatenate(pieces, axis=1), blocks[row, col], preferred_element_type=jnp.float32
            )
            if step < steps - 1:
                value = (summed - cheb_center * own.astype(jnp.float32)) * (
                    (1.0 if step == 0 else 2.0) / cheb_half
                )
                if step > 0:
                    value = value - exts[step - 1][half][row + 1, col + 1].astype(jnp.float32)
                value = jnp.where(lanes < counts[col, row], value, 0.0)
            else:
                value = jnp.where(lanes < counts[col, row], summed, 0.0)
            made.append(value.astype(own.dtype))
        for (row, col), value in zip(places, made):
            if step < steps - 1:
                exts[step + 1][half][row + 1, col + 1] = value
            else:
                images[row, col] = value

    def loop(count, body):
        def run(index, carry):
            body(index)
            return carry

        lax.fori_loop(0, count, run, 0)

    group = 2 if rows % 2 == 0 else 1

    def inner(step, half, wanted):
        def body(index):
            update(step, half, [(1 + index * group + i, col) for i in range(group) for col in wanted])

        loop((rows - 2) // group, body)

    def add_ritz(half):
        def body(row):
            right = jnp.concatenate([images[row, col] for col in range(cols)], axis=1)
            totals[halves + half] += lax.dot_general(wide(row), right, contract, preferred_element_type=jnp.float32)

        loop(rows, body)

    def sum_copy(which, stage, shift):
        digit, peers = sum_partners[stage]
        other, device = peers[shift]
        landing = arrived[which][stage].at[digit]
        return pltpu.make_async_remote_copy(
            src_ref=outgoing.at[which, other] if stage == 0 else landing,
            dst_ref=landing,
            send_sem=sum_send.at[which, stage, shift],
            recv_sem=sum_recv.at[which, stage, shift],
            device_id=device,
            device_id_type=MESH,
        )

    def send_stage(which, stage):
        for shift in range(stages[stage][2] - 1):
            sum_copy(which, stage, shift).start()

    def begin_sum(which):
        for block in range(band_count):
            outgoing[which, block, pl.ds(0, owned)] = totals[which, pl.ds(block * owned, owned)].astype(
                outgoing.dtype
            )
        send_stage(which, 0)
        mine = sum_partners[0][0]
        arrived[which][0][mine] = outgoing[which, mine]

    def finish_stage(which, stage):
        for shift in range(stages[stage][2] - 1):
            sum_copy(which, stage, shift).wait()
        ref = arrived[which][stage]
        total = ref[0].astype(jnp.float32)
        for slot in range(1, stages[stage][2]):
            total = total + ref[slot].astype(jnp.float32)
        if stage + 1 < len(stages):
            arrived[which][stage + 1][sum_partners[stage + 1][0]] = total.astype(ref.dtype)
            send_stage(which, stage + 1)
        else:
            scale = 3.0 / (rows * cols * elem_count * band_count * basis)
            (gram_ref, ritz_ref)[which // halves][:, pl.ds(which % halves * part, part)] = total[:owned] * scale

    out_copies = []
    for step in range(steps):
        for half in range(halves):
            for which in chosen("vertical"):
                halo(step, half, which).wait()
            for which in chosen("near"):
                halo(step, half, which).start()
            for which in chosen("far", "sideways", "near"):
                halo(step, half, which).wait()
            if step == 0 and half == 0:
                for copy in h_loads:
                    copy.wait()
            for row in (0, rows - 1):
                update(step, half, [(row, col) for col in range(cols)])
            if step < steps - 1:
                for which in chosen("vertical", "far"):
                    halo(step + 1, half, which).start()
            inner(step, half, (0, cols - 1))
            if step < steps - 1:
                for which in chosen("sideways"):
                    halo(step + 1, half, which).start()
            inner(step, half, range(1, cols - 1))
            if step == steps - 2:
                out_copies.append(
                    pltpu.make_async_copy(
                        exts[steps - 1][half].at[pl.ds(1, rows), pl.ds(1, cols)],
                        out_ref.at[:, :, pl.ds(half * part, part)],
                        out_sem.at[half],
                    )
                )
                out_copies[-1].start()
            if step == steps - 1:
                add_ritz(half)
                begin_sum(halves + half)
                if half < len(stages) - 1:
                    for which in range(halves):
                        finish_stage(which, half)
        if step == steps - 2:

            def gram_body(row, carry):
                left = wide(row)
                for half in range(halves):
                    right = left[half * part : (half + 1) * part]
                    totals[half] += lax.dot_general(left, right, contract, preferred_element_type=jnp.float32)
                return carry

            lax.fori_loop(0, rows, gram_body, 0)
            for half in range(halves):
                begin_sum(half)

    for stage in range(len(stages)):
        for which in range(2 * halves):
            if which >= halves or stage >= min(halves, len(stages) - 1):
                finish_stage(which, stage)
    for copy in out_copies:
        copy.wait()


def hand_on(*refs):
    count = (len(refs) - 1) // 3
    copies = []
    for source, target, stage in zip(refs[:count], refs[count : 2 * count], refs[2 * count : -1]):
        if len(source.shape) == 2:
            copies.append((source, target, stage))
        else:
            copies.extend((source.at[row], target.at[row], stage.at[row]) for row in range(source.shape[0]))
    loads = [pltpu.make_async_copy(a, c, refs[-1].at[0, i]) for i, (a, b, c) in enumerate(copies)]
    stores = [pltpu.make_async_copy(c, b, refs[-1].at[1, i]) for i, (a, b, c) in enumerate(copies)]
    for load in loads:
        load.start()
    for load, store in zip(loads, stores):
        load.wait()
        store.start()
    for store in stores:
        store.wait()


def on_device(elem_count, band_count, basis_counts, neighbour_codes, x_block, h_self, h_near):
    rows, cols, columns, basis = x_block.shape
    neighbours = neighbour_codes.shape[2]
    near = h_near.reshape(rows, cols, neighbours * basis, basis)
    ext = pltpu.VMEM((rows + 2, cols + 2, columns // halves, basis), x_block.dtype)
    whole = pl.BlockSpec(memory_space=pltpu.VMEM)
    owned = columns // band_count
    padded = -(-owned // 16) * 16
    share = jax.ShapeDtypeStruct((owned, columns), jnp.float32)
    radices = [band_count] + [radix for _, radix in digits(elem_count)]
    landing = [pltpu.VMEM((radix, padded, columns // halves), jnp.bfloat16) for radix in radices]
    anywhere = pl.BlockSpec(memory_space=pl.ANY)
    results = pl.pallas_call(
        functools.partial(kernel, elem_count, band_count),
        out_shape=(jax.ShapeDtypeStruct(x_block.shape, x_block.dtype), share, share),
        in_specs=[anywhere] * 5,
        out_specs=(anywhere, whole, whole),
        scratch_shapes=[ext] * (steps * halves)
        + [
            pltpu.VMEM((rows, cols, (neighbours + 1) * basis, basis), h_self.dtype),
            pltpu.VMEM((rows, cols, columns // halves, basis), x_block.dtype),
            pltpu.VMEM((2 * halves, columns, columns // halves), jnp.float32),
            pltpu.SMEM((cols, rows), jnp.int32),
            pltpu.SMEM((neighbours, cols, rows), jnp.int32),
            pltpu.SemaphoreType.DMA((steps, halves, 2 * len(ways))),
            pltpu.SemaphoreType.DMA((steps, halves, 2 * len(ways))),
            pltpu.SemaphoreType.DMA((halves + 4,)),
            pltpu.SemaphoreType.DMA((halves,)),
            pltpu.VMEM((2 * halves, band_count, padded, columns // halves), jnp.bfloat16),
            pltpu.SemaphoreType.DMA((2 * halves, len(radices), max(radices) - 1)),
            pltpu.SemaphoreType.DMA((2 * halves, len(radices), max(radices) - 1)),
        ]
        + landing * (2 * halves),
        compiler_params=pltpu.CompilerParams(
            collective_id=0, has_side_effects=True, vmem_limit_bytes=60 * 1024 * 1024
        ),
    )(basis_counts.T, neighbour_codes.transpose(2, 1, 0), x_block, h_self, near)
    return pl.pallas_call(
        hand_on,
        out_shape=tuple(jax.ShapeDtypeStruct(result.shape, result.dtype) for result in results),
        in_specs=[anywhere] * len(results),
        out_specs=(anywhere,) * len(results),
        scratch_shapes=[pltpu.VMEM(result.shape, result.dtype) for result in results]
        + [pltpu.SemaphoreType.DMA((2, rows + 2))],
        compiler_params=pltpu.CompilerParams(vmem_limit_bytes=60 * 1024 * 1024),
    )(*results)


def solution(mesh):
    in_specs = (
        P("elem", "band"),
        P("elem", "band", None),
        P("elem", "band", None, None),
        P("elem", "band", None, None),
        P("elem", "band", None, None, None),
    )
    out_specs = (P("elem", "band", None, None), P("band", None), P("band", None))
    return jax.shard_map(
        functools.partial(on_device, mesh.shape["elem"], mesh.shape["band"]),
        mesh=mesh,
        in_specs=in_specs,
        out_specs=out_specs,
        check_vma=False,
    )
```

```python
import functools

import jax
import jax.numpy as jnp
from jax import lax
from jax.experimental import pallas as pl
from jax.experimental.pallas import tpu as pltpu
from jax.sharding import PartitionSpec as P

MESH = pl.DeviceIdType.MESH
cheb_center = 0.25
cheb_half = 1.5
steps = 4
halves = 2
ways = ("vertical", "far", "near", "sideways")


def edge(shift, count):
    if shift == 0:
        return 1, 1, count
    return (count, 0, 1) if shift > 0 else (1, count + 1, 1)


def digits(count):
    found, stride = [], 1
    while stride < count:
        left = count // stride
        radix = 2 if left % 4 and left % 2 == 0 or stride == 1 and left % 2 == 0 else 4 if left % 4 == 0 else left
        found.append((stride, radix))
        stride *= radix
    return found


def kernel(elem_count, band_count, counts_ref, codes_ref, x_ref, self_ref, near_ref, out_ref, gram_ref, ritz_ref, *scratch):
    exts = [scratch[step * halves : (step + 1) * halves] for step in range(steps)]
    (
        blocks, images, totals, counts, codes, send_sem, recv_sem, load_sem, out_sem,
        outgoing, sum_send, sum_recv, *stage_refs
    ) = scratch[steps * halves :]
    neighbours, cols, rows = codes_ref.shape
    columns, basis = x_ref.shape[2:]
    part = columns // halves
    depth = near_ref.shape[2]
    owned = columns // band_count
    padded = outgoing.shape[2]
    stages = [("band", 1, band_count)] + [("elem", stride, radix) for stride, radix in digits(elem_count)]
    arrived = [stage_refs[m * len(stages) : (m + 1) * len(stages)] for m in range(2 * halves)]

    my_elem, my_band = lax.axis_index("elem"), lax.axis_index("band")
    odd = lax.rem(my_band, 2)
    inward, outward = 1 - 2 * odd, 2 * odd - 1
    moves = [(way, shift) for way in ways for shift in (-1, 1)]

    def device_at(a, b):
        return lax.rem(my_elem + a + elem_count, elem_count), lax.rem(my_band + b + band_count, band_count)

    partners = [device_at(a, b) for a in (-1, 0, 1) for b in (-1, 0, 1) if (a, b) != (0, 0)]

    small_loads = [
        pltpu.make_async_copy(counts_ref, counts, load_sem.at[halves + 2]),
        pltpu.make_async_copy(codes_ref, codes, load_sem.at[halves + 3]),
    ]
    x_loads = [
        pltpu.make_async_copy(
            x_ref.at[:, :, pl.ds(half * part, part)],
            exts[0][half].at[pl.ds(1, rows), pl.ds(1, cols)],
            load_sem.at[half],
        )
        for half in range(halves)
    ]
    h_loads = [
        pltpu.make_async_copy(near_ref, blocks.at[:, :, pl.ds(0, depth)], load_sem.at[halves]),
        pltpu.make_async_copy(self_ref, blocks.at[:, :, pl.ds(depth, basis)], load_sem.at[halves + 1]),
    ]
    for copy in small_loads + x_loads + h_loads:
        copy.start()

    sum_partners = []
    for axis, stride, radix in stages:
        mine = my_band if axis == "band" else my_elem
        digit = lax.rem(mine // stride, radix)
        peers = []
        for shift in range(1, radix):
            other = lax.rem(digit + shift, radix)
            moved = mine + (other - digit) * stride
            peers.append((other, (my_elem, moved) if axis == "band" else (moved, my_band)))
        sum_partners.append((digit, peers))

    greeted = partners + [device for _, peers in sum_partners for _, device in peers]
    barrier = pltpu.get_barrier_semaphore()
    for partner in greeted:
        pl.semaphore_signal(barrier, inc=1, device_id=partner, device_id_type=MESH)
    pl.semaphore_wait(barrier, len(greeted))
    for copy in small_loads:
        copy.wait()

    lanes = lax.broadcasted_iota(jnp.int32, (part, basis), 1)

    def halo(step, half, which, piece=None):
        way, shift = moves[which]
        first_col, some_cols = (1, cols) if piece is None else (1 + piece * (cols // pieces), cols // pieces)
        first_row, some_rows = (1, rows) if piece is None else (1 + piece * (rows // pieces), rows // pieces)
        ext = exts[step][half]
        if way == "vertical":
            start, landing, length = edge(shift, rows)
            src = ext.at[pl.ds(start, length), pl.ds(first_col, some_cols)]
            dst = ext.at[pl.ds(landing, length), pl.ds(first_col, some_cols)]
            device = device_at(shift, 0)
        elif way == "sideways":
            start, landing, length = edge(shift, cols)
            src = ext.at[pl.ds(first_row, some_rows), pl.ds(start, length)]
            dst = ext.at[pl.ds(first_row, some_rows), pl.ds(landing, length)]
            device = device_at(0, shift)
        elif way == "far":
            start, landing, length = edge(shift, rows)
            src = ext.at[pl.ds(start, length), pl.ds(1 + odd * (cols - 1), 1)]
            dst = ext.at[pl.ds(landing, length), pl.ds((1 - odd) * (cols + 1), 1)]
            device = device_at(shift, outward)
        else:
            row = 0 if shift < 0 else rows + 1
            src = ext.at[pl.ds(row, 1), pl.ds(cols - odd * (cols - 1), 1)]
            dst = ext.at[pl.ds(row, 1), pl.ds(odd * (cols + 1), 1)]
            device = device_at(0, inward)
        return pltpu.make_async_remote_copy(
            src_ref=src,
            dst_ref=dst,
            send_sem=send_sem.at[step, half, which],
            recv_sem=recv_sem.at[step, half, which],
            device_id=device,
            device_id_type=MESH,
        )

    pieces = cols if rows % cols == 0 else 1

    def send_halo(step, half):
        for which in chosen("far"):
            halo(step, half, which).start()
        for piece in range(pieces):
            for sideways, vertical in zip(chosen("sideways"), chosen("vertical")):
                halo(step, half, sideways, piece).start()
                halo(step, half, vertical, piece).start()

    def chosen(*wanted):
        return [index for index, (way, shift) in enumerate(moves) if way in wanted]

    for half in range(halves):
        x_loads[half].wait()
        ext = exts[0][half]

        def clear(row, carry, ext=ext):
            for col in range(cols):
                held = ext[row + 1, col + 1]
                ext[row + 1, col + 1] = jnp.where(
                    lanes < counts[col, row], held.astype(jnp.float32), 0.0
                ).astype(held.dtype)
            return carry

        lax.fori_loop(0, rows, clear, 0)
        send_halo(0, half)
    totals[...] = jnp.zeros_like(totals)
    outgoing[...] = jnp.zeros_like(outgoing)

    contract = (((1,), (1,)), ((), ()))

    def wide(row):
        return jnp.concatenate(
            [
                jnp.concatenate([exts[steps - 1][half][row + 1, col + 1] for half in range(halves)], axis=0)
                for col in range(cols)
            ],
            axis=1,
        )

    def update(step, half, places):
        ext = exts[step][half]
        made = []
        for row, col in places:
            operands = []
            for k in range(neighbours):
                code = codes[k, col, row]
                a = (code * 11) >> 5
                operands.append(ext[row + a, col + code - 3 * a])
            own = ext[row + 1, col + 1]
            operands.append(own)
            summed = jnp.dot(
                jnp.concatenate(operands, axis=1), blocks[row, col], preferred_element_type=jnp.float32
            )
            if step < steps - 1:
                value = (summed - cheb_center * own.astype(jnp.float32)) * (
                    (1.0 if step == 0 else 2.0) / cheb_half
                )
                if step > 0:
                    value = value - exts[step - 1][half][row + 1, col + 1].astype(jnp.float32)
                value = jnp.where(lanes < counts[col, row], value, 0.0)
            else:
                value = jnp.where(lanes < counts[col, row], summed, 0.0)
            made.append(value.astype(own.dtype))
        for (row, col), value in zip(places, made):
            if step < steps - 1:
                exts[step + 1][half][row + 1, col + 1] = value
            else:
                images[row, col] = value

    def loop(count, body):
        def run(index, carry):
            body(index)
            return carry

        lax.fori_loop(0, count, run, 0)

    group = 2 if rows % 2 == 0 else 1

    def inner(step, half, wanted):
        def body(index):
            update(step, half, [(1 + index * group + i, col) for i in range(group) for col in wanted])

        loop((rows - 2) // group, body)

    def add_ritz(half):
        def body(row):
            right = jnp.concatenate([images[row, col] for col in range(cols)], axis=1)
            totals[halves + half] += lax.dot_general(wide(row), right, contract, preferred_element_type=jnp.float32)

        loop(rows, body)

    def sum_copy(which, stage, shift):
        digit, peers = sum_partners[stage]
        other, device = peers[shift]
        landing = arrived[which][stage].at[digit]
        return pltpu.make_async_remote_copy(
            src_ref=outgoing.at[which, other] if stage == 0 else landing,
            dst_ref=landing,
            send_sem=sum_send.at[which, stage, shift],
            recv_sem=sum_recv.at[which, stage, shift],
            device_id=device,
            device_id_type=MESH,
        )

    def send_stage(which, stage):
        for shift in range(stages[stage][2] - 1):
            sum_copy(which, stage, shift).start()

    def begin_sum(which):
        for block in range(band_count):
            outgoing[which, block, pl.ds(0, owned)] = totals[which, pl.ds(block * owned, owned)].astype(
                outgoing.dtype
            )
        send_stage(which, 0)
        mine = sum_partners[0][0]
        arrived[which][0][mine] = outgoing[which, mine]

    def finish_stage(which, stage):
        for shift in range(stages[stage][2] - 1):
            sum_copy(which, stage, shift).wait()
        ref = arrived[which][stage]
        total = ref[0].astype(jnp.float32)
        for slot in range(1, stages[stage][2]):
            total = total + ref[slot].astype(jnp.float32)
        if stage + 1 < len(stages):
            arrived[which][stage + 1][sum_partners[stage + 1][0]] = total.astype(ref.dtype)
            send_stage(which, stage + 1)
        else:
            scale = 3.0 / (rows * cols * elem_count * band_count * basis)
            (gram_ref, ritz_ref)[which // halves][:, pl.ds(which % halves * part, part)] = total[:owned] * scale

    out_copies = []
    for step in range(steps):
        for half in range(halves):
            for which in chosen("vertical"):
                halo(step, half, which).wait()
            for which in chosen("near"):
                halo(step, half, which).start()
            for which in chosen("far", "sideways", "near"):
                halo(step, half, which).wait()
            if step == 0 and half == 0:
                for copy in h_loads:
                    copy.wait()
            for row in (0, rows - 1):
                update(step, half, [(row, col) for col in range(cols)])
            inner(step, half, (0, cols - 1))
            if step < steps - 1:
                send_halo(step + 1, half)
            inner(step, half, range(1, cols - 1))
            if step == steps - 2:
                out_copies.append(
                    pltpu.make_async_copy(
                        exts[steps - 1][half].at[pl.ds(1, rows), pl.ds(1, cols)],
                        out_ref.at[:, :, pl.ds(half * part, part)],
                        out_sem.at[half],
                    )
                )
                out_copies[-1].start()
            if step == steps - 1:
                add_ritz(half)
                begin_sum(halves + half)
                if half < len(stages) - 1:
                    for which in range(halves):
                        finish_stage(which, half)
        if step == steps - 2:

            def gram_body(row, carry):
                left = wide(row)
                for half in range(halves):
                    right = left[half * part : (half + 1) * part]
                    totals[half] += lax.dot_general(left, right, contract, preferred_element_type=jnp.float32)
                return carry

            lax.fori_loop(0, rows, gram_body, 0)
            for half in range(halves):
                begin_sum(half)

    for stage in range(len(stages)):
        for which in range(2 * halves):
            if which >= halves or stage >= min(halves, len(stages) - 1):
                finish_stage(which, stage)
    for copy in out_copies:
        copy.wait()


def hand_on(*refs):
    count = (len(refs) - 1) // 3
    copies = []
    for source, target, stage in zip(refs[:count], refs[count : 2 * count], refs[2 * count : -1]):
        if len(source.shape) == 2:
            copies.append((source, target, stage))
        else:
            copies.extend((source.at[row], target.at[row], stage.at[row]) for row in range(source.shape[0]))
    loads = [pltpu.make_async_copy(a, c, refs[-1].at[0, i]) for i, (a, b, c) in enumerate(copies)]
    stores = [pltpu.make_async_copy(c, b, refs[-1].at[1, i]) for i, (a, b, c) in enumerate(copies)]
    for load in loads:
        load.start()
    for load, store in zip(loads, stores):
        load.wait()
        store.start()
    for store in stores:
        store.wait()


def on_device(elem_count, band_count, basis_counts, neighbour_codes, x_block, h_self, h_near):
    rows, cols, columns, basis = x_block.shape
    neighbours = neighbour_codes.shape[2]
    near = h_near.reshape(rows, cols, neighbours * basis, basis)
    ext = pltpu.VMEM((rows + 2, cols + 2, columns // halves, basis), x_block.dtype)
    whole = pl.BlockSpec(memory_space=pltpu.VMEM)
    owned = columns // band_count
    padded = -(-owned // 16) * 16
    share = jax.ShapeDtypeStruct((owned, columns), jnp.float32)
    radices = [band_count] + [radix for _, radix in digits(elem_count)]
    landing = [pltpu.VMEM((radix, padded, columns // halves), jnp.bfloat16) for radix in radices]
    anywhere = pl.BlockSpec(memory_space=pl.ANY)
    results = pl.pallas_call(
        functools.partial(kernel, elem_count, band_count),
        out_shape=(jax.ShapeDtypeStruct(x_block.shape, x_block.dtype), share, share),
        in_specs=[anywhere] * 5,
        out_specs=(anywhere, whole, whole),
        scratch_shapes=[ext] * (steps * halves)
        + [
            pltpu.VMEM((rows, cols, (neighbours + 1) * basis, basis), h_self.dtype),
            pltpu.VMEM((rows, cols, columns // halves, basis), x_block.dtype),
            pltpu.VMEM((2 * halves, columns, columns // halves), jnp.float32),
            pltpu.SMEM((cols, rows), jnp.int32),
            pltpu.SMEM((neighbours, cols, rows), jnp.int32),
            pltpu.SemaphoreType.DMA((steps, halves, 2 * len(ways))),
            pltpu.SemaphoreType.DMA((steps, halves, 2 * len(ways))),
            pltpu.SemaphoreType.DMA((halves + 4,)),
            pltpu.SemaphoreType.DMA((halves,)),
            pltpu.VMEM((2 * halves, band_count, padded, columns // halves), jnp.bfloat16),
            pltpu.SemaphoreType.DMA((2 * halves, len(radices), max(radices) - 1)),
            pltpu.SemaphoreType.DMA((2 * halves, len(radices), max(radices) - 1)),
        ]
        + landing * (2 * halves),
        compiler_params=pltpu.CompilerParams(
            collective_id=0, has_side_effects=True, vmem_limit_bytes=60 * 1024 * 1024
        ),
    )(basis_counts.T, neighbour_codes.transpose(2, 1, 0), x_block, h_self, near)
    return pl.pallas_call(
        hand_on,
        out_shape=tuple(jax.ShapeDtypeStruct(result.shape, result.dtype) for result in results),
        in_specs=[anywhere] * len(results),
        out_specs=(anywhere,) * len(results),
        scratch_shapes=[pltpu.VMEM(result.shape, result.dtype) for result in results]
        + [pltpu.SemaphoreType.DMA((2, rows + 2))],
        compiler_params=pltpu.CompilerParams(vmem_limit_bytes=60 * 1024 * 1024),
    )(*results)


def solution(mesh):
    in_specs = (
        P("elem", "band"),
        P("elem", "band", None),
        P("elem", "band", None, None),
        P("elem", "band", None, None),
        P("elem", "band", None, None, None),
    )
    out_specs = (P("elem", "band", None, None), P("band", None), P("band", None))
    return jax.shard_map(
        functools.partial(on_device, mesh.shape["elem"], mesh.shape["band"]),
        mesh=mesh,
        in_specs=in_specs,
        out_specs=out_specs,
        check_vma=False,
    )
```

```python
import functools

import jax
import jax.numpy as jnp
from jax import lax
from jax.experimental import pallas as pl
from jax.experimental.pallas import tpu as pltpu
from jax.sharding import PartitionSpec as P

MESH = pl.DeviceIdType.MESH
cheb_center = 0.25
cheb_half = 1.5
steps = 4
halves = 2
ways = ("vertical", "far", "near", "sideways")


def edge(shift, count):
    if shift == 0:
        return 1, 1, count
    return (count, 0, 1) if shift > 0 else (1, count + 1, 1)


def digits(count):
    found, stride = [], 1
    while stride < count:
        left = count // stride
        radix = 2 if left % 4 and left % 2 == 0 or stride == 1 and left % 2 == 0 else 4 if left % 4 == 0 else left
        found.append((stride, radix))
        stride *= radix
    return found


def kernel(elem_count, band_count, counts_ref, codes_ref, x_ref, self_ref, near_ref, out_ref, gram_ref, ritz_ref, *scratch):
    exts = [scratch[step * halves : (step + 1) * halves] for step in range(steps)]
    (
        blocks, images, totals, counts, codes, send_sem, recv_sem, load_sem, out_sem,
        outgoing, sum_send, sum_recv, *stage_refs
    ) = scratch[steps * halves :]
    neighbours, cols, rows = codes_ref.shape
    columns, basis = x_ref.shape[2:]
    part = columns // halves
    depth = near_ref.shape[2]
    owned = columns // band_count
    padded = outgoing.shape[2]
    stages = [("band", 1, band_count)] + [("elem", stride, radix) for stride, radix in digits(elem_count)]
    arrived = [stage_refs[m * len(stages) : (m + 1) * len(stages)] for m in range(2 * halves)]

    my_elem, my_band = lax.axis_index("elem"), lax.axis_index("band")
    odd = lax.rem(my_band, 2)
    inward, outward = 1 - 2 * odd, 2 * odd - 1
    moves = [(way, shift) for way in ways for shift in (-1, 1)]

    def device_at(a, b):
        return lax.rem(my_elem + a + elem_count, elem_count), lax.rem(my_band + b + band_count, band_count)

    partners = [device_at(a, b) for a in (-1, 0, 1) for b in (-1, 0, 1) if (a, b) != (0, 0)]

    small_loads = [
        pltpu.make_async_copy(counts_ref, counts, load_sem.at[halves + 2]),
        pltpu.make_async_copy(codes_ref, codes, load_sem.at[halves + 3]),
    ]
    x_loads = [
        pltpu.make_async_copy(
            x_ref.at[:, :, pl.ds(half * part, part)],
            exts[0][half].at[pl.ds(1, rows), pl.ds(1, cols)],
            load_sem.at[half],
        )
        for half in range(halves)
    ]
    h_loads = [
        pltpu.make_async_copy(near_ref, blocks.at[:, :, pl.ds(0, depth)], load_sem.at[halves]),
        pltpu.make_async_copy(self_ref, blocks.at[:, :, pl.ds(depth, basis)], load_sem.at[halves + 1]),
    ]
    for copy in small_loads + x_loads + h_loads:
        copy.start()

    sum_partners = []
    for axis, stride, radix in stages:
        mine = my_band if axis == "band" else my_elem
        digit = lax.rem(mine // stride, radix)
        peers = []
        for shift in range(1, radix):
            other = lax.rem(digit + shift, radix)
            moved = mine + (other - digit) * stride
            peers.append((other, (my_elem, moved) if axis == "band" else (moved, my_band)))
        sum_partners.append((digit, peers))

    greeted = partners + [device for _, peers in sum_partners for _, device in peers]
    barrier = pltpu.get_barrier_semaphore()
    for partner in greeted:
        pl.semaphore_signal(barrier, inc=1, device_id=partner, device_id_type=MESH)
    pl.semaphore_wait(barrier, len(greeted))
    for copy in small_loads:
        copy.wait()

    lanes = lax.broadcasted_iota(jnp.int32, (part, basis), 1)

    def halo(step, half, which):
        way, shift = moves[which]
        ext = exts[step][half]
        if way == "vertical":
            start, landing, length = edge(shift, rows)
            src = ext.at[pl.ds(start, length), pl.ds(1, cols)]
            dst = ext.at[pl.ds(landing, length), pl.ds(1, cols)]
            device = device_at(shift, 0)
        elif way == "sideways":
            start, landing, length = edge(shift, cols)
            src = ext.at[pl.ds(1, rows), pl.ds(start, length)]
            dst = ext.at[pl.ds(1, rows), pl.ds(landing, length)]
            device = device_at(0, shift)
        elif way == "far":
            start, landing, length = edge(shift, rows)
            src = ext.at[pl.ds(start, length), pl.ds(1 + odd * (cols - 1), 1)]
            dst = ext.at[pl.ds(landing, length), pl.ds((1 - odd) * (cols + 1), 1)]
            device = device_at(shift, outward)
        else:
            row = 0 if shift < 0 else rows + 1
            src = ext.at[pl.ds(row, 1), pl.ds(cols - odd * (cols - 1), 1)]
            dst = ext.at[pl.ds(row, 1), pl.ds(odd * (cols + 1), 1)]
            device = device_at(0, inward)
        return pltpu.make_async_remote_copy(
            src_ref=src,
            dst_ref=dst,
            send_sem=send_sem.at[step, half, which],
            recv_sem=recv_sem.at[step, half, which],
            device_id=device,
            device_id_type=MESH,
        )

    def chosen(*wanted):
        return [index for index, (way, shift) in enumerate(moves) if way in wanted]

    for half in range(halves):
        x_loads[half].wait()
        ext = exts[0][half]

        def clear(row, carry, ext=ext):
            for col in range(cols):
                held = ext[row + 1, col + 1]
                ext[row + 1, col + 1] = jnp.where(
                    lanes < counts[col, row], held.astype(jnp.float32), 0.0
                ).astype(held.dtype)
            return carry

        lax.fori_loop(0, rows, clear, 0)
        for which in chosen("vertical", "far", "sideways"):
            halo(0, half, which).start()
    totals[...] = jnp.zeros_like(totals)
    outgoing[...] = jnp.zeros_like(outgoing)

    contract = (((1,), (1,)), ((), ()))

    def wide(row):
        return jnp.concatenate(
            [
                jnp.concatenate([exts[steps - 1][half][row + 1, col + 1] for half in range(halves)], axis=0)
                for col in range(cols)
            ],
            axis=1,
        )

    def update(step, half, places):
        ext = exts[step][half]
        made = []
        for row, col in places:
            pieces = []
            for k in range(neighbours):
                code = codes[k, col, row]
                a = (code * 11) >> 5
                pieces.append(ext[row + a, col + code - 3 * a])
            own = ext[row + 1, col + 1]
            pieces.append(own)
            summed = jnp.dot(
                jnp.concatenate(pieces, axis=1), blocks[row, col], preferred_element_type=jnp.float32
            )
            if step < steps - 1:
                value = (summed - cheb_center * own.astype(jnp.float32)) * (
                    (1.0 if step == 0 else 2.0) / cheb_half
                )
                if step > 0:
                    value = value - exts[step - 1][half][row + 1, col + 1].astype(jnp.float32)
                value = jnp.where(lanes < counts[col, row], value, 0.0)
            else:
                value = jnp.where(lanes < counts[col, row], summed, 0.0)
            made.append(value.astype(own.dtype))
        for (row, col), value in zip(places, made):
            if step < steps - 1:
                exts[step + 1][half][row + 1, col + 1] = value
            else:
                images[row, col] = value

    def loop(count, body):
        def run(index, carry):
            body(index)
            return carry

        lax.fori_loop(0, count, run, 0)

    group = 2 if rows % 2 == 0 else 1

    def inner(step, half, wanted):
        def body(index):
            update(step, half, [(1 + index * group + i, col) for i in range(group) for col in wanted])

        loop((rows - 2) // group, body)

    def add_ritz(half):
        def body(row):
            right = jnp.concatenate([images[row, col] for col in range(cols)], axis=1)
            totals[halves + half] += lax.dot_general(wide(row), right, contract, preferred_element_type=jnp.float32)

        loop(rows, body)

    def sum_copy(which, stage, shift):
        digit, peers = sum_partners[stage]
        other, device = peers[shift]
        landing = arrived[which][stage].at[digit]
        return pltpu.make_async_remote_copy(
            src_ref=outgoing.at[which, other] if stage == 0 else landing,
            dst_ref=landing,
            send_sem=sum_send.at[which, stage, shift],
            recv_sem=sum_recv.at[which, stage, shift],
            device_id=device,
            device_id_type=MESH,
        )

    def send_stage(which, stage):
        for shift in range(stages[stage][2] - 1):
            sum_copy(which, stage, shift).start()

    def begin_sum(which):
        for block in range(band_count):
            outgoing[which, block, pl.ds(0, owned)] = totals[which, pl.ds(block * owned, owned)].astype(
                outgoing.dtype
            )
        send_stage(which, 0)
        mine = sum_partners[0][0]
        arrived[which][0][mine] = outgoing[which, mine]

    def finish_stage(which, stage):
        for shift in range(stages[stage][2] - 1):
            sum_copy(which, stage, shift).wait()
        ref = arrived[which][stage]
        total = ref[0].astype(jnp.float32)
        for slot in range(1, stages[stage][2]):
            total = total + ref[slot].astype(jnp.float32)
        if stage + 1 < len(stages):
            arrived[which][stage + 1][sum_partners[stage + 1][0]] = total.astype(ref.dtype)
            send_stage(which, stage + 1)
        else:
            scale = 3.0 / (rows * cols * elem_count * band_count * basis)
            (gram_ref, ritz_ref)[which // halves][:, pl.ds(which % halves * part, part)] = total[:owned] * scale

    def forward_corners(step, half):
        for which in chosen("vertical"):
            halo(step, half, which).wait()
        for which in chosen("near"):
            halo(step, half, which).start()

    out_copies = []
    forward_corners(0, 0)
    for step in range(steps):
        for half in range(halves):
            for which in chosen("far", "sideways", "near"):
                halo(step, half, which).wait()
            if step == 0 and half == 0:
                for copy in h_loads:
                    copy.wait()
            for row in (0, rows - 1):
                update(step, half, [(row, col) for col in range(cols)])
            if step < steps - 1:
                for which in chosen("vertical", "far"):
                    halo(step + 1, half, which).start()
            inner(step, half, (0, cols - 1))
            if step < steps - 1:
                for which in chosen("sideways"):
                    halo(step + 1, half, which).start()
            if half + 1 < halves:
                forward_corners(step, half + 1)
            elif step < steps - 1:
                forward_corners(step + 1, 0)
            inner(step, half, range(1, cols - 1))
            if step == steps - 2:
                out_copies.append(
                    pltpu.make_async_copy(
                        exts[steps - 1][half].at[pl.ds(1, rows), pl.ds(1, cols)],
                        out_ref.at[:, :, pl.ds(half * part, part)],
                        out_sem.at[half],
                    )
                )
                out_copies[-1].start()
            if step == steps - 1:
                add_ritz(half)
                begin_sum(halves + half)
                if half < len(stages) - 1:
                    for which in range(halves):
                        finish_stage(which, half)
        if step == steps - 2:

            def gram_body(row, carry):
                left = wide(row)
                for half in range(halves):
                    right = left[half * part : (half + 1) * part]
                    totals[half] += lax.dot_general(left, right, contract, preferred_element_type=jnp.float32)
                return carry

            lax.fori_loop(0, rows, gram_body, 0)
            for half in range(halves):
                begin_sum(half)

    for stage in range(len(stages)):
        for which in range(2 * halves):
            if which >= halves or stage >= min(halves, len(stages) - 1):
                finish_stage(which, stage)
    for copy in out_copies:
        copy.wait()


def hand_on(*refs):
    count = (len(refs) - 1) // 3
    copies = []
    for source, target, stage in zip(refs[:count], refs[count : 2 * count], refs[2 * count : -1]):
        if len(source.shape) == 2:
            copies.append((source, target, stage))
        else:
            copies.extend((source.at[row], target.at[row], stage.at[row]) for row in range(source.shape[0]))
    loads = [pltpu.make_async_copy(a, c, refs[-1].at[0, i]) for i, (a, b, c) in enumerate(copies)]
    stores = [pltpu.make_async_copy(c, b, refs[-1].at[1, i]) for i, (a, b, c) in enumerate(copies)]
    for load in loads:
        load.start()
    for load, store in zip(loads, stores):
        load.wait()
        store.start()
    for store in stores:
        store.wait()


def on_device(elem_count, band_count, basis_counts, neighbour_codes, x_block, h_self, h_near):
    rows, cols, columns, basis = x_block.shape
    neighbours = neighbour_codes.shape[2]
    near = h_near.reshape(rows, cols, neighbours * basis, basis)
    ext = pltpu.VMEM((rows + 2, cols + 2, columns // halves, basis), x_block.dtype)
    whole = pl.BlockSpec(memory_space=pltpu.VMEM)
    owned = columns // band_count
    padded = -(-owned // 16) * 16
    share = jax.ShapeDtypeStruct((owned, columns), jnp.float32)
    radices = [band_count] + [radix for _, radix in digits(elem_count)]
    landing = [pltpu.VMEM((radix, padded, columns // halves), jnp.bfloat16) for radix in radices]
    anywhere = pl.BlockSpec(memory_space=pl.ANY)
    results = pl.pallas_call(
        functools.partial(kernel, elem_count, band_count),
        out_shape=(jax.ShapeDtypeStruct(x_block.shape, x_block.dtype), share, share),
        in_specs=[anywhere] * 5,
        out_specs=(anywhere, whole, whole),
        scratch_shapes=[ext] * (steps * halves)
        + [
            pltpu.VMEM((rows, cols, (neighbours + 1) * basis, basis), h_self.dtype),
            pltpu.VMEM((rows, cols, columns // halves, basis), x_block.dtype),
            pltpu.VMEM((2 * halves, columns, columns // halves), jnp.float32),
            pltpu.SMEM((cols, rows), jnp.int32),
            pltpu.SMEM((neighbours, cols, rows), jnp.int32),
            pltpu.SemaphoreType.DMA((steps, halves, 2 * len(ways))),
            pltpu.SemaphoreType.DMA((steps, halves, 2 * len(ways))),
            pltpu.SemaphoreType.DMA((halves + 4,)),
            pltpu.SemaphoreType.DMA((halves,)),
            pltpu.VMEM((2 * halves, band_count, padded, columns // halves), jnp.bfloat16),
            pltpu.SemaphoreType.DMA((2 * halves, len(radices), max(radices) - 1)),
            pltpu.SemaphoreType.DMA((2 * halves, len(radices), max(radices) - 1)),
        ]
        + landing * (2 * halves),
        compiler_params=pltpu.CompilerParams(
            collective_id=0, has_side_effects=True, vmem_limit_bytes=60 * 1024 * 1024
        ),
    )(basis_counts.T, neighbour_codes.transpose(2, 1, 0), x_block, h_self, near)
    return pl.pallas_call(
        hand_on,
        out_shape=tuple(jax.ShapeDtypeStruct(result.shape, result.dtype) for result in results),
        in_specs=[anywhere] * len(results),
        out_specs=(anywhere,) * len(results),
        scratch_shapes=[pltpu.VMEM(result.shape, result.dtype) for result in results]
        + [pltpu.SemaphoreType.DMA((2, rows + 2))],
        compiler_params=pltpu.CompilerParams(vmem_limit_bytes=60 * 1024 * 1024),
    )(*results)


def solution(mesh):
    in_specs = (
        P("elem", "band"),
        P("elem", "band", None),
        P("elem", "band", None, None),
        P("elem", "band", None, None),
        P("elem", "band", None, None, None),
    )
    out_specs = (P("elem", "band", None, None), P("band", None), P("band", None))
    return jax.shard_map(
        functools.partial(on_device, mesh.shape["elem"], mesh.shape["band"]),
        mesh=mesh,
        in_specs=in_specs,
        out_specs=out_specs,
        check_vma=False,
    )
```

```python
import functools

import jax
import jax.numpy as jnp
from jax import lax
from jax.experimental import pallas as pl
from jax.experimental.pallas import tpu as pltpu
from jax.sharding import PartitionSpec as P

MESH = pl.DeviceIdType.MESH
cheb_center = 0.25
cheb_half = 1.5
steps = 4
halves = 2
ways = ("vertical", "far", "near", "sideways")


def edge(shift, count):
    if shift == 0:
        return 1, 1, count
    return (count, 0, 1) if shift > 0 else (1, count + 1, 1)


def digits(count):
    found, stride = [], 1
    while stride < count:
        left = count // stride
        radix = 2 if left % 4 and left % 2 == 0 or stride == 1 and left % 2 == 0 else 4 if left % 4 == 0 else left
        found.append((stride, radix))
        stride *= radix
    return found


def kernel(elem_count, band_count, counts_ref, codes_ref, x_ref, self_ref, near_ref, out_ref, gram_ref, ritz_ref, *scratch):
    exts = [scratch[step * halves : (step + 1) * halves] for step in range(steps)]
    (
        blocks, images, totals, counts, codes, send_sem, recv_sem, load_sem, out_sem,
        outgoing, sum_send, sum_recv, *stage_refs
    ) = scratch[steps * halves :]
    neighbours, cols, rows = codes_ref.shape
    columns, basis = x_ref.shape[2:]
    part = columns // halves
    depth = near_ref.shape[2]
    owned = columns // band_count
    padded = outgoing.shape[2]
    stages = [("band", 1, band_count)] + [("elem", stride, radix) for stride, radix in digits(elem_count)]
    arrived = [stage_refs[m * len(stages) : (m + 1) * len(stages)] for m in range(2 * halves)]

    my_elem, my_band = lax.axis_index("elem"), lax.axis_index("band")
    odd = lax.rem(my_band, 2)
    inward, outward = 1 - 2 * odd, 2 * odd - 1
    moves = [(way, shift) for way in ways for shift in (-1, 1)]

    def device_at(a, b):
        return lax.rem(my_elem + a + elem_count, elem_count), lax.rem(my_band + b + band_count, band_count)

    partners = [device_at(a, b) for a in (-1, 0, 1) for b in (-1, 0, 1) if (a, b) != (0, 0)]

    small_loads = [
        pltpu.make_async_copy(counts_ref, counts, load_sem.at[halves + 2]),
        pltpu.make_async_copy(codes_ref, codes, load_sem.at[halves + 3]),
    ]
    x_loads = [
        pltpu.make_async_copy(
            x_ref.at[:, :, pl.ds(half * part, part)],
            exts[0][half].at[pl.ds(1, rows), pl.ds(1, cols)],
            load_sem.at[half],
        )
        for half in range(halves)
    ]
    h_loads = [
        pltpu.make_async_copy(near_ref, blocks.at[:, :, pl.ds(0, depth)], load_sem.at[halves]),
        pltpu.make_async_copy(self_ref, blocks.at[:, :, pl.ds(depth, basis)], load_sem.at[halves + 1]),
    ]
    for copy in small_loads + x_loads + h_loads:
        copy.start()

    sum_partners = []
    for axis, stride, radix in stages:
        mine = my_band if axis == "band" else my_elem
        digit = lax.rem(mine // stride, radix)
        peers = []
        for shift in range(1, radix):
            other = lax.rem(digit + shift, radix)
            moved = mine + (other - digit) * stride
            peers.append((other, (my_elem, moved) if axis == "band" else (moved, my_band)))
        sum_partners.append((digit, peers))

    greeted = partners + [device for _, peers in sum_partners for _, device in peers]
    barrier = pltpu.get_barrier_semaphore()
    for partner in greeted:
        pl.semaphore_signal(barrier, inc=1, device_id=partner, device_id_type=MESH)
    pl.semaphore_wait(barrier, len(greeted))
    for copy in small_loads:
        copy.wait()

    lanes = lax.broadcasted_iota(jnp.int32, (part, basis), 1)

    def halo(step, half, which):
        way, shift = moves[which]
        ext = exts[step][half]
        if way == "vertical":
            start, landing, length = edge(shift, rows)
            src = ext.at[pl.ds(start, length), pl.ds(1, cols)]
            dst = ext.at[pl.ds(landing, length), pl.ds(1, cols)]
            device = device_at(shift, 0)
        elif way == "sideways":
            start, landing, length = edge(shift, cols)
            src = ext.at[pl.ds(1, rows), pl.ds(start, length)]
            dst = ext.at[pl.ds(1, rows), pl.ds(landing, length)]
            device = device_at(0, shift)
        elif way == "far":
            row = 0 if shift < 0 else rows + 1
            src = ext.at[pl.ds(row, 1), pl.ds(1 + odd * (cols - 1), 1)]
            dst = ext.at[pl.ds(row, 1), pl.ds((1 - odd) * (cols + 1), 1)]
            device = device_at(0, outward)
        else:
            row = 0 if shift < 0 else rows + 1
            src = ext.at[pl.ds(row, 1), pl.ds(cols - odd * (cols - 1), 1)]
            dst = ext.at[pl.ds(row, 1), pl.ds(odd * (cols + 1), 1)]
            device = device_at(0, inward)
        return pltpu.make_async_remote_copy(
            src_ref=src,
            dst_ref=dst,
            send_sem=send_sem.at[step, half, which],
            recv_sem=recv_sem.at[step, half, which],
            device_id=device,
            device_id_type=MESH,
        )

    def chosen(*wanted):
        return [index for index, (way, shift) in enumerate(moves) if way in wanted]

    for half in range(halves):
        x_loads[half].wait()
        ext = exts[0][half]

        def clear(row, carry, ext=ext):
            for col in range(cols):
                held = ext[row + 1, col + 1]
                ext[row + 1, col + 1] = jnp.where(
                    lanes < counts[col, row], held.astype(jnp.float32), 0.0
                ).astype(held.dtype)
            return carry

        lax.fori_loop(0, rows, clear, 0)
        for which in chosen("vertical", "sideways"):
            halo(0, half, which).start()
    totals[...] = jnp.zeros_like(totals)
    outgoing[...] = jnp.zeros_like(outgoing)

    contract = (((1,), (1,)), ((), ()))

    def wide(row):
        return jnp.concatenate(
            [
                jnp.concatenate([exts[steps - 1][half][row + 1, col + 1] for half in range(halves)], axis=0)
                for col in range(cols)
            ],
            axis=1,
        )

    def update(step, half, places):
        ext = exts[step][half]
        made = []
        for row, col in places:
            pieces = []
            for k in range(neighbours):
                code = codes[k, col, row]
                a = (code * 11) >> 5
                pieces.append(ext[row + a, col + code - 3 * a])
            own = ext[row + 1, col + 1]
            pieces.append(own)
            summed = jnp.dot(
                jnp.concatenate(pieces, axis=1), blocks[row, col], preferred_element_type=jnp.float32
            )
            if step < steps - 1:
                value = (summed - cheb_center * own.astype(jnp.float32)) * (
                    (1.0 if step == 0 else 2.0) / cheb_half
                )
                if step > 0:
                    value = value - exts[step - 1][half][row + 1, col + 1].astype(jnp.float32)
                value = jnp.where(lanes < counts[col, row], value, 0.0)
            else:
                value = jnp.where(lanes < counts[col, row], summed, 0.0)
            made.append(value.astype(own.dtype))
        for (row, col), value in zip(places, made):
            if step < steps - 1:
                exts[step + 1][half][row + 1, col + 1] = value
            else:
                images[row, col] = value

    def loop(count, body):
        def run(index, carry):
            body(index)
            return carry

        lax.fori_loop(0, count, run, 0)

    group = 2 if rows % 2 == 0 else 1

    def inner(step, half, wanted):
        def body(index):
            update(step, half, [(1 + index * group + i, col) for i in range(group) for col in wanted])

        loop((rows - 2) // group, body)

    def add_ritz(half):
        def body(row):
            right = jnp.concatenate([images[row, col] for col in range(cols)], axis=1)
            totals[halves + half] += lax.dot_general(wide(row), right, contract, preferred_element_type=jnp.float32)

        loop(rows, body)

    def sum_copy(which, stage, shift):
        digit, peers = sum_partners[stage]
        other, device = peers[shift]
        landing = arrived[which][stage].at[digit]
        return pltpu.make_async_remote_copy(
            src_ref=outgoing.at[which, other] if stage == 0 else landing,
            dst_ref=landing,
            send_sem=sum_send.at[which, stage, shift],
            recv_sem=sum_recv.at[which, stage, shift],
            device_id=device,
            device_id_type=MESH,
        )

    def send_stage(which, stage):
        for shift in range(stages[stage][2] - 1):
            sum_copy(which, stage, shift).start()

    def begin_sum(which):
        for block in range(band_count):
            outgoing[which, block, pl.ds(0, owned)] = totals[which, pl.ds(block * owned, owned)].astype(
                outgoing.dtype
            )
        send_stage(which, 0)
        mine = sum_partners[0][0]
        arrived[which][0][mine] = outgoing[which, mine]

    def finish_stage(which, stage):
        for shift in range(stages[stage][2] - 1):
            sum_copy(which, stage, shift).wait()
        ref = arrived[which][stage]
        total = ref[0].astype(jnp.float32)
        for slot in range(1, stages[stage][2]):
            total = total + ref[slot].astype(jnp.float32)
        if stage + 1 < len(stages):
            arrived[which][stage + 1][sum_partners[stage + 1][0]] = total.astype(ref.dtype)
            send_stage(which, stage + 1)
        else:
            scale = 3.0 / (rows * cols * elem_count * band_count * basis)
            (gram_ref, ritz_ref)[which // halves][:, pl.ds(which % halves * part, part)] = total[:owned] * scale

    out_copies = []
    for step in range(steps):
        for half in range(halves):
            for which in chosen("vertical"):
                halo(step, half, which).wait()
            for which in chosen("far", "near"):
                halo(step, half, which).start()
            for which in chosen("far", "sideways", "near"):
                halo(step, half, which).wait()
            if step == 0 and half == 0:
                for copy in h_loads:
                    copy.wait()
            for row in (0, rows - 1):
                update(step, half, [(row, col) for col in range(cols)])
            if step < steps - 1:
                for which in chosen("vertical"):
                    halo(step + 1, half, which).start()
            inner(step, half, (0, cols - 1))
            if step < steps - 1:
                for which in chosen("sideways"):
                    halo(step + 1, half, which).start()
            inner(step, half, range(1, cols - 1))
            if step == steps - 2:
                out_copies.append(
                    pltpu.make_async_copy(
                        exts[steps - 1][half].at[pl.ds(1, rows), pl.ds(1, cols)],
                        out_ref.at[:, :, pl.ds(half * part, part)],
                        out_sem.at[half],
                    )
                )
                out_copies[-1].start()
            if step == steps - 1:
                add_ritz(half)
                begin_sum(halves + half)
                if half < len(stages) - 1:
                    for which in range(halves):
                        finish_stage(which, half)
        if step == steps - 2:

            def gram_body(row, carry):
                left = wide(row)
                for half in range(halves):
                    right = left[half * part : (half + 1) * part]
                    totals[half] += lax.dot_general(left, right, contract, preferred_element_type=jnp.float32)
                return carry

            lax.fori_loop(0, rows, gram_body, 0)
            for half in range(halves):
                begin_sum(half)

    for stage in range(len(stages)):
        for which in range(2 * halves):
            if which >= halves or stage >= min(halves, len(stages) - 1):
                finish_stage(which, stage)
    for copy in out_copies:
        copy.wait()


def hand_on(*refs):
    count = (len(refs) - 1) // 3
    copies = []
    for source, target, stage in zip(refs[:count], refs[count : 2 * count], refs[2 * count : -1]):
        if len(source.shape) == 2:
            copies.append((source, target, stage))
        else:
            copies.extend((source.at[row], target.at[row], stage.at[row]) for row in range(source.shape[0]))
    loads = [pltpu.make_async_copy(a, c, refs[-1].at[0, i]) for i, (a, b, c) in enumerate(copies)]
    stores = [pltpu.make_async_copy(c, b, refs[-1].at[1, i]) for i, (a, b, c) in enumerate(copies)]
    for load in loads:
        load.start()
    for load, store in zip(loads, stores):
        load.wait()
        store.start()
    for store in stores:
        store.wait()


def on_device(elem_count, band_count, basis_counts, neighbour_codes, x_block, h_self, h_near):
    rows, cols, columns, basis = x_block.shape
    neighbours = neighbour_codes.shape[2]
    near = h_near.reshape(rows, cols, neighbours * basis, basis)
    ext = pltpu.VMEM((rows + 2, cols + 2, columns // halves, basis), x_block.dtype)
    whole = pl.BlockSpec(memory_space=pltpu.VMEM)
    owned = columns // band_count
    padded = -(-owned // 16) * 16
    share = jax.ShapeDtypeStruct((owned, columns), jnp.float32)
    radices = [band_count] + [radix for _, radix in digits(elem_count)]
    landing = [pltpu.VMEM((radix, padded, columns // halves), jnp.bfloat16) for radix in radices]
    anywhere = pl.BlockSpec(memory_space=pl.ANY)
    results = pl.pallas_call(
        functools.partial(kernel, elem_count, band_count),
        out_shape=(jax.ShapeDtypeStruct(x_block.shape, x_block.dtype), share, share),
        in_specs=[anywhere] * 5,
        out_specs=(anywhere, whole, whole),
        scratch_shapes=[ext] * (steps * halves)
        + [
            pltpu.VMEM((rows, cols, (neighbours + 1) * basis, basis), h_self.dtype),
            pltpu.VMEM((rows, cols, columns // halves, basis), x_block.dtype),
            pltpu.VMEM((2 * halves, columns, columns // halves), jnp.float32),
            pltpu.SMEM((cols, rows), jnp.int32),
            pltpu.SMEM((neighbours, cols, rows), jnp.int32),
            pltpu.SemaphoreType.DMA((steps, halves, 2 * len(ways))),
            pltpu.SemaphoreType.DMA((steps, halves, 2 * len(ways))),
            pltpu.SemaphoreType.DMA((halves + 4,)),
            pltpu.SemaphoreType.DMA((halves,)),
            pltpu.VMEM((2 * halves, band_count, padded, columns // halves), jnp.bfloat16),
            pltpu.SemaphoreType.DMA((2 * halves, len(radices), max(radices) - 1)),
            pltpu.SemaphoreType.DMA((2 * halves, len(radices), max(radices) - 1)),
        ]
        + landing * (2 * halves),
        compiler_params=pltpu.CompilerParams(
            collective_id=0, has_side_effects=True, vmem_limit_bytes=60 * 1024 * 1024
        ),
    )(basis_counts.T, neighbour_codes.transpose(2, 1, 0), x_block, h_self, near)
    return pl.pallas_call(
        hand_on,
        out_shape=tuple(jax.ShapeDtypeStruct(result.shape, result.dtype) for result in results),
        in_specs=[anywhere] * len(results),
        out_specs=(anywhere,) * len(results),
        scratch_shapes=[pltpu.VMEM(result.shape, result.dtype) for result in results]
        + [pltpu.SemaphoreType.DMA((2, rows + 2))],
        compiler_params=pltpu.CompilerParams(vmem_limit_bytes=60 * 1024 * 1024),
    )(*results)


def solution(mesh):
    in_specs = (
        P("elem", "band"),
        P("elem", "band", None),
        P("elem", "band", None, None),
        P("elem", "band", None, None),
        P("elem", "band", None, None, None),
    )
    out_specs = (P("elem", "band", None, None), P("band", None), P("band", None))
    return jax.shard_map(
        functools.partial(on_device, mesh.shape["elem"], mesh.shape["band"]),
        mesh=mesh,
        in_specs=in_specs,
        out_specs=out_specs,
        check_vma=False,
    )
```
